32 devices in a mesh: dom: 8 (over z, x), feat: 4 (over y, core).
Axes of the slice: x: 2, y: 2, z: 4, core: 2. Of those that a mesh axis runs over, the one named last changes fastest.
Arguments:
- embed: bfloat16 [256, 8192], P('feat', 'dom'), may hold values from -6 to 6
- weight: bfloat16 [256, 256], P('feat'), may hold values from -0.375 to 0.375
- cotangent: bfloat16 [256, 8192], P('feat', 'dom'), may hold values from -6 to 6
- edge_masks: int32 [768, 128, 128], P('dom'), may hold values 0 or 1
- tile_rows: int32 [768], P('dom'), may hold values from 0 to 7
- tile_owner: int32 [768, 1], P('dom'), may hold values from 0 to 7; in each aligned block of 96 rows (0 to 95, 96 to 191, ...) at most 24 rows name the same one
- tile_sub: int32 [768], P('dom'), may hold values from 0 to 7
Outputs:
- output: bfloat16 [256, 8192], P('feat', 'dom')
- embed_grad: float32 [256, 8192], P('feat', 'dom')
- weight_grad: float32 [256, 256], P('feat')
The draws below stay inside these ranges and needn't reach their ends.
Inputs may be any that keep to these rules, and one draw needn't show every extreme that they name: `tile_owner`: among the 96 tiles of one index of dom no owner is named more than 24 times, a bound that some block reaches.
All inputs are finite; a program needn't handle non-finite values. No bound on the sum of `edge_masks` on one device may be relied on, other than what follows from the above.
Results may differ from the reference program's by a relative error of at most 0.0059.
Values may be sent and summed in bfloat16 or wider, within the bound.
A program may use at most 64 MiB of HBM per device.

```python
import math
import jax
import jax.numpy as jnp
import numpy as np
from jax import lax

H = 256
BLK = 128
NB_DEV = 8
TILES_DEV = 96
TILES = 768
NBLK = 64
NODES = 8192
CAP = 24
N_DOM = 8


def place_ends(values, stream_key, low, high):
    extent = values.shape
    spot = [jax.random.randint(jax.random.fold_in(stream_key, axis), (), 0, extent[axis]) for axis in range(len(extent))]
    values = values.at[tuple(spot)].set(low)
    longest = extent.index(max(extent))
    spot[longest] = (spot[longest] + 1) % extent[longest]
    return values.at[tuple(spot)].set(high)


def level_of(own_key, shape, split, least, top_value):
    gain = 1.0
    for position, blocks in split:
        draws = jax.random.uniform(jax.random.fold_in(jax.random.fold_in(own_key, 6), position), (blocks,), jnp.float32, least / len(split), top_value / len(split))
        gain = gain * jnp.repeat(jnp.exp(draws), shape[position] // blocks).reshape((-1,) + (1,) * (len(shape) - 1 - position))
    return gain


def shared_out(rng, own, number, rows, amount, top, bound, skew):
    sequence = jax.random.permutation(rng, amount)
    crowded, common = load_shares(amount, rows * top, bound, skew, True), load_shares(amount, rows * top, bound, skew, False)
    places = jnp.arange(amount)

    def named(lengths, turn):
        used = int((lengths > 0).sum())
        fixed = max(1, used // 4)
        passed = fixed + (places - fixed + turn * (used - fixed)) % max(1, amount - fixed)
        return jnp.zeros((amount,), jnp.int32).at[sequence[jnp.where(places < fixed, places, passed)]].set(jnp.asarray(lengths, jnp.int32))

    lengths = jnp.where(number % 4 == 0, named(crowded, number // 4), named(common, number - number // 4 - 1))
    mixed = jax.random.permutation(jax.random.fold_in(own, 3), amount)
    donor, receiver = mixed[0:amount // 2 * 2:2], mixed[1:amount // 2 * 2:2]
    slack = jnp.minimum(lengths[donor] - 1, bound - lengths[receiver]) // 2
    slack = jnp.where((donor == sequence[0]) | (receiver == sequence[0]) | (lengths[receiver] == 0), 0, jnp.maximum(slack, 0))
    passed = jax.random.randint(jax.random.fold_in(own, 4), (amount // 2,), 0, 1 << 20) % (slack + 1)
    lengths = lengths.at[donor].add(-passed).at[receiver].add(passed)
    items = jnp.searchsorted(jnp.cumsum(lengths), jnp.arange(rows * top), side="right").astype(jnp.int32)
    table = items.reshape(top, rows).T
    table = table[jax.random.permutation(jax.random.fold_in(own, 1), rows)]
    turn = jax.random.randint(jax.random.fold_in(own, 2), (rows, 1), 0, top)
    return jnp.take_along_axis(table, (jnp.arange(top)[None, :] + turn) % top, axis=1)


def load_shares(amount, total, most, skew, full):
    portions = [(1 << 20) // math.isqrt(grade ** skew) + 1 for grade in range(1, amount + 1)]
    largest = most if full else min(most, max(-(-total // amount), total * portions[0] // sum(portions)))
    least = 1 if total - largest >= amount - 1 else 0
    given, spare = [largest] + [least] * (amount - 1), total - largest - least * (amount - 1)
    while spare > 0:
        candidates = [i for i in range(1, amount) if given[i] < largest] or [i for i in range(1, amount) if given[i] < most]
        whole, left = sum([portions[i] for i in candidates]), spare
        for i in candidates:
            extra = min(most - given[i], max(1, left * portions[i] // whole), spare)
            given[i] = given[i] + extra
            spare = spare - extra
    return np.array(given)


def gaussian(key, extent, deviation, limit, split=(), kind=jnp.bfloat16):
    drawn = jax.random.normal(key, extent, jnp.float32) * deviation
    if len(split) > 0:
        drawn = level_of(key, extent, split, -0.22, 0.18) * drawn
    return jnp.clip(drawn, min=-limit, max=limit).astype(kind)


def setup_inputs(seed: int = 0) -> dict:
    arg_keys = jax.random.split(jax.random.key(seed), 8)
    embed = gaussian(arg_keys[0], (H, NODES), 1.0, 6.0, ((0, 4), (1, 8)))
    weight = gaussian(arg_keys[1], (H, H), H ** -0.5, 0.375, ((0, 4),))
    cotangent = gaussian(arg_keys[2], (H, NODES), 1.0, 6.0, ((0, 4), (1, 8)))
    edge_masks = place_ends((jax.random.randint(arg_keys[3], (TILES, BLK, BLK), 0, 16) < 1).astype(jnp.int32), jax.random.fold_in(arg_keys[3], 1), 0, 1)
    tile_rows = place_ends(jax.random.randint(arg_keys[4], (TILES,), 0, NB_DEV), jax.random.fold_in(arg_keys[4], 1), 0, NB_DEV - 1).astype(jnp.int32)
    tile_owner_keys = jax.random.split(jax.random.fold_in(arg_keys[5], 1), TILES // TILES_DEV)
    tile_owner_turns = jax.random.permutation(jax.random.fold_in(arg_keys[5], 3), TILES // TILES_DEV)
    tile_owner = jax.vmap(lambda own, number: shared_out(jax.random.fold_in(arg_keys[5], 2), own, number, TILES_DEV, N_DOM, 1, CAP, 2))(tile_owner_keys, tile_owner_turns).reshape((TILES, 1))
    tile_sub = place_ends(jax.random.randint(arg_keys[6], (TILES,), 0, NB_DEV), jax.random.fold_in(arg_keys[6], 1), 0, NB_DEV - 1).astype(jnp.int32)
    return {"embed": embed, "weight": weight, "cotangent": cotangent, "edge_masks": edge_masks, "tile_rows": tile_rows, "tile_owner": tile_owner, "tile_sub": tile_sub}


def reference(embed, weight, cotangent, edge_masks, tile_rows, tile_owner, tile_sub):
    blocks = embed.reshape(H, NBLK, BLK)
    tile_masks = edge_masks.reshape(N_DOM, TILES_DEV, BLK, BLK)
    row_ids = tile_rows.reshape(N_DOM, TILES_DEV).astype(jnp.int32)
    col_ids = (tile_owner[:, 0] * NB_DEV + tile_sub).astype(jnp.int32).reshape(N_DOM, TILES_DEV)
    block_range = jnp.arange(NB_DEV, dtype=jnp.int32)

    def forward_block(packed):
        mask_one, row_one, col_one = packed
        fetched = jnp.take(blocks, col_one, axis=1).astype(jnp.float32)
        contrib = jnp.einsum('htj,tij->hti', fetched, mask_one.astype(jnp.float32))
        row_onehot = (row_one[:, None] == block_range[None, :]).astype(jnp.float32)
        neighbour = jnp.einsum('hti,tr->hri', contrib, row_onehot, precision=lax.Precision.HIGHEST)
        row_int = (row_one[:, None] == block_range[None, :]).astype(jnp.int32)
        counts = lax.optimization_barrier(jnp.sum(mask_one, axis=2)).astype(jnp.int32)
        degree = jnp.dot(row_int.T, counts)
        inv_root = 1.0 / jnp.sqrt(1.0 + degree.astype(jnp.float32))
        return (neighbour, inv_root)
    neighbours, roots = lax.map(forward_block, (tile_masks, row_ids, col_ids))
    neighbour = jnp.transpose(neighbours, (1, 0, 2, 3)).reshape(H, NODES)
    inv_root = roots.reshape(NODES)
    aggregate = (embed.astype(jnp.float32) + neighbour * inv_root[None, :]).astype(jnp.bfloat16)
    pre_act = jnp.dot(weight.T, aggregate, preferred_element_type=jnp.float32)
    gate_vals = jax.nn.sigmoid(pre_act)
    output = (pre_act * gate_vals).astype(jnp.bfloat16)
    grad_pre = (cotangent.astype(jnp.float32) * gate_vals * (1.0 + pre_act * (1.0 - gate_vals))).astype(jnp.bfloat16)
    grad_agg = jnp.dot(weight, grad_pre, preferred_element_type=jnp.float32)
    weight_grad = jnp.dot(aggregate, grad_pre.T, preferred_element_type=jnp.float32) / math.sqrt(NODES)
    scaled_grad = (grad_agg * inv_root[None, :]).astype(jnp.bfloat16)
    scaled_parts = jnp.transpose(scaled_grad.reshape(H, N_DOM, NB_DEV, BLK), (1, 0, 2, 3))

    def backward_block(totals, packed):
        mask_one, row_one, col_one, grad_part = packed
        selected = jnp.take(grad_part, row_one, axis=1).astype(jnp.float32)
        partial_value = jnp.einsum('hti,tij->htj', selected, mask_one.astype(jnp.float32))
        totals = totals.at[:, col_one].add(partial_value)
        return (totals, None)
    start_totals = jnp.zeros((H, NBLK, BLK), jnp.float32)
    totals, unused = lax.scan(backward_block, start_totals, (tile_masks, row_ids, col_ids, scaled_parts))
    embed_grad = grad_agg + totals.reshape(H, NODES)
    return (output, embed_grad, weight_grad)
```

```python
import functools
import math

import jax
import jax.numpy as jnp
from jax import lax
from jax.experimental import pallas as pl
from jax.experimental.pallas import tpu as pltpu
from jax.sharding import PartitionSpec as P

MESH = pl.DeviceIdType.MESH
VMEM = pl.BlockSpec(memory_space=pltpu.VMEM)
SMEM = pl.BlockSpec(memory_space=pltpu.SMEM)
ANY = pl.BlockSpec(memory_space=pl.ANY)
ONES = 16
CHUNK = 16
VMEM_LIMIT = 56 * 1024 * 1024


def greet(dom_mates, feat_mates):
    barrier = pltpu.get_barrier_semaphore()
    for mate in dom_mates:
        pl.semaphore_signal(barrier, inc=1, device_id={"dom": mate}, device_id_type=MESH)
    for mate in feat_mates:
        pl.semaphore_signal(barrier, inc=1, device_id={"feat": mate}, device_id_type=MESH)
    pl.semaphore_wait(barrier, len(dom_mates) + len(feat_mates))


def send(src, dst, send_sem, recv_sem, **where):
    return pltpu.make_async_remote_copy(
        src_ref=src,
        dst_ref=dst,
        send_sem=send_sem,
        recv_sem=recv_sem,
        device_id=where,
        device_id_type=MESH,
    )


def places(n):
    me = lax.axis_index("dom")
    half = n // 2
    high, low = me // 2, lax.rem(me, 2)
    ahead = [lax.rem(high + k, half) for k in range(half)]
    behind = [lax.rem(high + half - k, half) for k in range(half)]
    return me, low, ahead, behind


def gather_kernel(
    n, f, embed, cot, weight, masks, gath, cot_all, w_all, masks_bf,
    raw, raw_sem, z_send, z_recv, x_send, x_recv, f_send, f_recv,
):
    me, low, ahead, behind = places(n)
    half = n // 2
    feat = lax.axis_index("feat")
    partner = me + 1 - 2 * low
    tiles = masks.shape[0]
    pieces = tiles // CHUNK
    loads = [
        pltpu.make_async_copy(
            masks.at[pl.ds(c * CHUNK, CHUNK)], raw.at[pl.ds(c * CHUNK, CHUNK)], raw_sem.at[c]
        )
        for c in range(pieces)
    ]
    for load in loads:
        load.start()
    feat_mates = [lax.rem(feat + k, f) for k in range(1, f)]
    greet([ahead[k] * 2 + low for k in range(1, half)] + [partner], feat_mates)
    z_copies = [
        send(embed, gath.at[me], z_send.at[k], z_recv.at[k], dom=ahead[k] * 2 + low)
        for k in range(1, half)
    ]
    x_copies = [send(embed, gath.at[me], x_send.at[0], x_recv.at[0], dom=partner)]
    for k in range(1, half):
        slot = gath.at[behind[k] * 2 + low]
        x_copies.append(send(slot, slot, x_send.at[k], x_recv.at[k], dom=partner))
    f_copies = []
    for k in range(1, f):
        f_copies.append(
            send(weight, w_all.at[feat], f_send.at[0, k], f_recv.at[0, k], feat=feat_mates[k - 1])
        )
        f_copies.append(
            send(cot, cot_all.at[feat], f_send.at[1, k], f_recv.at[1, k], feat=feat_mates[k - 1])
        )
    for copy in z_copies + x_copies[:1] + f_copies:
        copy.start()
    gath[me] = embed[...]
    cot_all[feat] = cot[...]
    w_all[feat] = weight[...]
    forwarded = 0
    for c in range(pieces):
        loads[c].wait()

        @pl.loop(c * CHUNK, (c + 1) * CHUNK)
        def _(t):
            masks_bf[t] = raw[t].astype(jnp.float32).astype(jnp.bfloat16)

        if c >= 2 and forwarded < half - 1:
            z_copies[forwarded].wait_recv()
            x_copies[forwarded + 1].start()
            forwarded += 1
    while forwarded < half - 1:
        z_copies[forwarded].wait_recv()
        x_copies[forwarded + 1].start()
        forwarded += 1
    for copy in f_copies + x_copies:
        copy.wait()
    for copy in z_copies:
        copy.wait_send()


def forward_kernel(rows, owner, sub, gath, masks_bf, embed, agg, inv_root, acc):
    tiles, block, _ = masks_bf.shape
    width, local_nodes = embed.shape
    blocks = local_nodes // block
    acc[...] = jnp.zeros_like(acc)
    ones = jnp.ones((ONES, block), jnp.bfloat16)

    def step(t, carry):
        columns = pl.ds(pl.multiple_of(sub[t] * block, block), block)
        taken = jnp.concatenate([gath[owner[t], :, columns], ones], axis=0)
        part = lax.dot_general(
            taken, masks_bf[t], (((1,), (1,)), ((), ())), preferred_element_type=jnp.float32
        )
        acc[rows[t]] += part
        return carry

    lax.fori_loop(0, tiles, step, 0, unroll=8)
    for b in range(blocks):
        columns = slice(b * block, (b + 1) * block)
        root = 1.0 / jnp.sqrt(1.0 + acc[b, width : width + 1, :])
        inv_root[:, columns] = root
        agg[:, columns] = (
            embed[:, columns].astype(jnp.float32) + acc[b, :width, :] * root
        ).astype(jnp.bfloat16)


def dense_kernel(
    f, agg, w_all, weight, cot_all, inv_root, out, grad_agg, scaled, w_terms,
    agg_all, out_all, f_send, f_recv,
):
    feat = lax.axis_index("feat")
    width, local_nodes = agg.shape
    full = f * width
    feat_mates = [lax.rem(feat + k, f) for k in range(1, f)]
    greet([], feat_mates)
    copies = [
        send(agg, agg_all.at[feat], f_send.at[k], f_recv.at[k], feat=feat_mates[k - 1])
        for k in range(1, f)
    ]
    for copy in copies:
        copy.start()
    agg_all[feat] = agg[...]
    whole_w = w_all[...].reshape(full, full)
    for copy in copies:
        copy.wait()
    step = min(256, local_nodes)
    w_terms[...] = jnp.zeros_like(w_terms)

    @pl.loop(0, local_nodes // step)
    def _(c):
        columns = pl.ds(pl.multiple_of(c * step, step), step)
        values = agg_all[:, :, columns].reshape(full, step)
        pre = lax.dot_general(
            whole_w, values, (((0,), (0,)), ((), ())), preferred_element_type=jnp.float32
        )
        gate = jax.nn.sigmoid(pre)
        out_all[:, :, columns] = (pre * gate).astype(jnp.bfloat16).reshape(f, width, step)
        cot = cot_all[:, :, columns].reshape(full, step).astype(jnp.float32)
        grad = (cot * gate * (1.0 + pre * (1.0 - gate))).astype(jnp.bfloat16)
        back = jnp.dot(weight[...], grad, preferred_element_type=jnp.float32)
        grad_agg[:, columns] = back
        scaled[:, columns] = (back * inv_root[:, columns]).astype(jnp.bfloat16)
        w_terms[...] += lax.dot_general(
            agg[:, columns], grad, (((1,), (1,)), ((), ())), preferred_element_type=jnp.float32
        )

    out[...] = out_all[feat]


def backward_kernel(rows, owner, sub, scaled, masks_bf, part, acc):
    tiles, block, _ = masks_bf.shape
    owners = acc.shape[0]

    @pl.loop(0, owners)
    def _(o):
        acc[o] = jnp.zeros_like(acc[o])

    def step(t, carry):
        taken = scaled[:, pl.ds(pl.multiple_of(rows[t] * block, block), block)]
        columns = pl.ds(pl.multiple_of(sub[t] * block, block), block)
        acc[owner[t], :, columns] += jnp.dot(
            taken, masks_bf[t], preferred_element_type=jnp.float32
        )
        return carry

    lax.fori_loop(0, tiles, step, 0, unroll=8)

    @pl.loop(0, owners)
    def _(o):
        part[o] = acc[o].astype(jnp.bfloat16)


def reduce_kernel(
    n, scale, part, grad_agg, w_terms, embed_grad, weight_grad,
    x_buf, z_out, z_buf, w_sum, w_buf, x_send, x_recv, z_send, z_recv, w_send, w_recv,
):
    me, low, ahead, behind = places(n)
    half = n // 2
    partner = me + 1 - 2 * low
    greet([ahead[k] * 2 + low for k in range(1, half)] + [partner], [])
    order = list(range(1, half)) + [0]
    x_copies = {
        k: send(part.at[ahead[k] * 2 + 1 - low], x_buf.at[k], x_send.at[k], x_recv.at[k], dom=partner)
        for k in order
    }
    z_copies = {
        k: send(z_out.at[k], z_buf.at[k], z_send.at[k], z_recv.at[k], dom=ahead[k] * 2 + low)
        for k in range(1, half)
    }
    rounds = n.bit_length() - 1
    w_copies = []
    for b in range(rounds):
        bit = lax.rem(me // (1 << b), 2)
        mate = me + (1 - 2 * bit) * (1 << b)
        src = w_terms if b == 0 else w_sum.at[b - 1]
        w_copies.append(send(src, w_buf.at[b], w_send.at[b], w_recv.at[b], dom=mate))
    w_copies[0].start()
    for k in order:
        x_copies[k].start()

    def w_round(b):
        w_copies[b].wait_recv()
        held = w_terms[...] if b == 0 else w_sum[b - 1]
        total = held + w_buf[b]
        if b == rounds - 1:
            weight_grad[...] = total * scale
        else:
            w_sum[b] = total
            w_copies[b + 1].start()

    done = 0
    for k in order:
        if done < rounds:
            w_round(done)
            done += 1
        x_copies[k].wait_recv()
        total = x_buf[k].astype(jnp.float32) + part[ahead[k] * 2 + low].astype(jnp.float32)
        if k:
            z_out[k] = total.astype(jnp.bfloat16)
            z_copies[k].start()
        else:
            embed_grad[...] = grad_agg[...] + total
    while done < rounds:
        w_round(done)
        done += 1
    for k in range(1, half):
        z_copies[k].wait_recv()
        embed_grad[...] += z_buf[k].astype(jnp.float32)
    for copy in list(x_copies.values()) + list(z_copies.values()) + w_copies:
        copy.wait_send()


def params(collective_id=None):
    if collective_id is None:
        return pltpu.CompilerParams(vmem_limit_bytes=VMEM_LIMIT)
    return pltpu.CompilerParams(
        collective_id=collective_id, has_side_effects=True, vmem_limit_bytes=VMEM_LIMIT
    )


def per_device(embed, weight, cotangent, edge_masks, tile_rows, tile_owner, tile_sub):
    width, local_nodes = embed.shape
    tiles, block, _ = edge_masks.shape
    blocks = local_nodes // block
    n = lax.axis_size("dom")
    f = lax.axis_size("feat")
    full = f * width
    half = n // 2
    rounds = n.bit_length() - 1
    bf, f32 = jnp.bfloat16, jnp.float32
    dma = pltpu.SemaphoreType.DMA
    owner = tile_owner.reshape(tiles)

    gath, cot_all, w_all, masks_bf = pl.pallas_call(
        functools.partial(gather_kernel, n, f),
        out_shape=(
            jax.ShapeDtypeStruct((n, width, local_nodes), bf),
            jax.ShapeDtypeStruct((f, width, local_nodes), bf),
            jax.ShapeDtypeStruct((f, width, full), bf),
            jax.ShapeDtypeStruct((tiles, block, block), bf),
        ),
        in_specs=[VMEM, VMEM, VMEM, ANY],
        out_specs=(VMEM,) * 4,
        scratch_shapes=[
            pltpu.VMEM((tiles, block, block), jnp.int32),
            dma((tiles // CHUNK,)),
            dma((half,)),
            dma((half,)),
            dma((half,)),
            dma((half,)),
            dma((2, f)),
            dma((2, f)),
        ],
        compiler_params=params(0),
        name="gather",
    )(embed, cotangent, weight, edge_masks)

    agg, inv_root = pl.pallas_call(
        forward_kernel,
        out_shape=(
            jax.ShapeDtypeStruct((width, local_nodes), bf),
            jax.ShapeDtypeStruct((1, local_nodes), f32),
        ),
        in_specs=[SMEM] * 3 + [VMEM] * 3,
        out_specs=(VMEM,) * 2,
        scratch_shapes=[pltpu.VMEM((blocks, width + ONES, block), f32)],
        compiler_params=params(),
        name="forward",
    )(tile_rows, owner, tile_sub, gath, masks_bf, embed)

    output, grad_agg, scaled, w_terms = pl.pallas_call(
        functools.partial(dense_kernel, f),
        out_shape=(
            jax.ShapeDtypeStruct((width, local_nodes), bf),
            jax.ShapeDtypeStruct((width, local_nodes), f32),
            jax.ShapeDtypeStruct((width, local_nodes), bf),
            jax.ShapeDtypeStruct((width, full), f32),
        ),
        in_specs=[VMEM] * 5,
        out_specs=(VMEM,) * 4,
        scratch_shapes=[
            pltpu.VMEM((f, width, local_nodes), bf),
            pltpu.VMEM((f, width, local_nodes), bf),
            dma((f,)),
            dma((f,)),
        ],
        compiler_params=params(1),
        name="dense",
    )(agg, w_all, weight, cot_all, inv_root)

    part = pl.pallas_call(
        backward_kernel,
        out_shape=jax.ShapeDtypeStruct((n, width, local_nodes), bf),
        in_specs=[SMEM] * 3 + [VMEM] * 2,
        out_specs=VMEM,
        scratch_shapes=[pltpu.VMEM((n, width, local_nodes), f32)],
        compiler_params=params(),
        name="backward",
    )(tile_rows, owner, tile_sub, scaled, masks_bf)

    embed_grad, weight_grad = pl.pallas_call(
        functools.partial(reduce_kernel, n, 1.0 / math.sqrt(n * local_nodes)),
        out_shape=(
            jax.ShapeDtypeStruct((width, local_nodes), f32),
            jax.ShapeDtypeStruct((width, full), f32),
        ),
        in_specs=[VMEM] * 3,
        out_specs=(VMEM,) * 2,
        scratch_shapes=[
            pltpu.VMEM((half, width, local_nodes), bf),
            pltpu.VMEM((half, width, local_nodes), bf),
            pltpu.VMEM((half, width, local_nodes), bf),
            pltpu.VMEM((rounds, width, full), f32),
            pltpu.VMEM((rounds, width, full), f32),
            dma((half,)),
            dma((half,)),
            dma((half,)),
            dma((half,)),
            dma((rounds,)),
            dma((rounds,)),
        ],
        compiler_params=params(2),
        name="reduce",
    )(part, grad_agg, w_terms)
    return (output, embed_grad, weight_grad)


def solution(mesh):
    in_specs = (
        P("feat", "dom"),
        P("feat", None),
        P("feat", "dom"),
        P("dom", None, None),
        P("dom"),
        P("dom", None),
        P("dom"),
    )
    out_specs = (P("feat", "dom"), P("feat", "dom"), P("feat", None))
    return jax.shard_map(
        per_device, mesh=mesh, in_specs=in_specs, out_specs=out_specs, check_vma=False
    )
```

```python
import functools
import math

import jax
import jax.numpy as jnp
from jax import lax
from jax.experimental import pallas as pl
from jax.experimental.pallas import tpu as pltpu
from jax.sharding import PartitionSpec as P

MESH = pl.DeviceIdType.MESH
VMEM = pl.BlockSpec(memory_space=pltpu.VMEM)
SMEM = pl.BlockSpec(memory_space=pltpu.SMEM)
ANY = pl.BlockSpec(memory_space=pl.ANY)
ONES = 16
CHUNK = 16
PIECES = 4
VMEM_LIMIT = 56 * 1024 * 1024


def greet(dom_mates, feat_mates):
    barrier = pltpu.get_barrier_semaphore()
    for mate in dom_mates:
        pl.semaphore_signal(barrier, inc=1, device_id={"dom": mate}, device_id_type=MESH)
    for mate in feat_mates:
        pl.semaphore_signal(barrier, inc=1, device_id={"feat": mate}, device_id_type=MESH)
    pl.semaphore_wait(barrier, len(dom_mates) + len(feat_mates))


def send(src, dst, send_sem, recv_sem, **where):
    return pltpu.make_async_remote_copy(
        src_ref=src,
        dst_ref=dst,
        send_sem=send_sem,
        recv_sem=recv_sem,
        device_id=where,
        device_id_type=MESH,
    )


def places(axis, n):
    me = lax.axis_index(axis)
    half = n // 2
    high, low = me // 2, lax.rem(me, 2)
    ahead = [lax.rem(high + k, half) for k in range(half)]
    behind = [lax.rem(high + half - k, half) for k in range(half)]
    return me, low, me + 1 - 2 * low, ahead, behind


def mates(axis, n):
    _, low, partner, ahead, _ = places(axis, n)
    return [ahead[k] * 2 + low for k in range(1, n // 2)] + [partner]


class Gather:
    def __init__(self, axis, n, src, dst, sems, pieces):
        me, low, partner, ahead, behind = places(axis, n)
        half = n // 2
        rows = src.shape[0] // pieces
        self.first, self.second, self.own = [], [], []
        for p in range(pieces):
            part = pl.ds(p * rows, rows)
            for k in range(1, half):
                self.first.append(
                    send(
                        src.at[part], dst.at[me, part], sems.at[0, k, p], sems.at[1, k, p],
                        **{axis: ahead[k] * 2 + low},
                    )
                )
                slot = dst.at[behind[k] * 2 + low, part]
                self.second.append(
                    send(slot, slot, sems.at[2, k, p], sems.at[3, k, p], **{axis: partner})
                )
            self.own.append(
                send(
                    src.at[part], dst.at[me, part], sems.at[2, 0, p], sems.at[3, 0, p],
                    **{axis: partner},
                )
            )
        self.at = 0

    def start(self):
        per = len(self.first) // len(self.own)
        for p, copy in enumerate(self.own):
            copy.start()
            for other in self.first[p * per : (p + 1) * per]:
                other.start()

    def forward(self, count):
        for _ in range(count):
            if self.at < len(self.first):
                self.first[self.at].wait_recv()
                self.second[self.at].start()
                self.at += 1

    def finish(self):
        self.forward(len(self.first))
        for copy in self.first:
            copy.wait_send()
        for copy in self.own + self.second:
            copy.wait()


def gather_kernel(
    n, f, embed, cot, weight, masks, gath, cot_all, w_all, masks_bf,
    raw, narrow, raw_sem, bf_sem, e_sems, c_sems, w_sems,
):
    tiles = masks.shape[0]
    pieces = tiles // CHUNK
    spans = [pl.ds(c * CHUNK, CHUNK) for c in range(pieces)]
    loads = [
        pltpu.make_async_copy(masks.at[s], raw.at[s], raw_sem.at[c]) for c, s in enumerate(spans)
    ]
    stores = [
        pltpu.make_async_copy(narrow.at[s], masks_bf.at[s], bf_sem.at[c])
        for c, s in enumerate(spans)
    ]
    for load in loads:
        load.start()
    greet(mates("dom", n), mates("feat", f))
    e_gather = Gather("dom", n, embed, gath, e_sems, PIECES)
    c_gather = Gather("feat", f, cot, cot_all, c_sems, PIECES)
    w_gather = Gather("feat", f, weight, w_all, w_sems, 1)
    for gather in (e_gather, w_gather, c_gather):
        gather.start()
    gath[lax.axis_index("dom")] = embed[...]
    cot_all[lax.axis_index("feat")] = cot[...]
    w_all[lax.axis_index("feat")] = weight[...]
    for c in range(pieces):
        loads[c].wait()

        @pl.loop(c * CHUNK, (c + 1) * CHUNK)
        def _(t):
            narrow[t] = raw[t].astype(jnp.float32).astype(jnp.bfloat16)

        stores[c].start()
        if c >= 2:
            e_gather.forward(2)
    w_gather.forward(1)
    e_gather.forward(2)
    c_gather.forward(PIECES)
    for gather in (e_gather, w_gather, c_gather):
        gather.finish()
    for store in stores:
        store.wait()


def forward_kernel(rows, owner, sub, gath, masks_bf, embed, agg, inv_root, acc):
    tiles, block, _ = masks_bf.shape
    width, local_nodes = embed.shape
    blocks = local_nodes // block
    acc[...] = jnp.zeros_like(acc)
    ones = jnp.ones((ONES, block), jnp.bfloat16)

    def step(t, carry):
        columns = pl.ds(pl.multiple_of(sub[t] * block, block), block)
        taken = jnp.concatenate([gath[owner[t], :, columns], ones], axis=0)
        part = lax.dot_general(
            taken, masks_bf[t], (((1,), (1,)), ((), ())), preferred_element_type=jnp.float32
        )
        acc[rows[t]] += part
        return carry

    lax.fori_loop(0, tiles, step, 0, unroll=8)
    for b in range(blocks):
        columns = slice(b * block, (b + 1) * block)
        root = 1.0 / jnp.sqrt(1.0 + acc[b, width : width + 1, :])
        inv_root[:, columns] = root
        agg[:, columns] = (
            embed[:, columns].astype(jnp.float32) + acc[b, :width, :] * root
        ).astype(jnp.bfloat16)


def share_kernel(f, agg, agg_all, sems):
    greet([], mates("feat", f))
    gather = Gather("feat", f, agg, agg_all, sems, PIECES)
    gather.start()
    agg_all[lax.axis_index("feat")] = agg[...]
    gather.finish()


def backward_kernel(
    f, rows, owner, sub, feat, agg, agg_all, w_all, weight, cot_all, inv_root, masks_bf,
    out, grad_agg, w_terms, part, scaled, out_all, acc,
):
    width, local_nodes = agg.shape
    full = f * width
    whole_w = w_all[...].reshape(full, full)
    step = min(256, local_nodes)
    w_terms[...] = jnp.zeros_like(w_terms)

    @pl.loop(0, local_nodes // step)
    def _(c):
        columns = pl.ds(pl.multiple_of(c * step, step), step)
        values = agg_all[:, :, columns].reshape(full, step)
        pre = lax.dot_general(
            whole_w, values, (((0,), (0,)), ((), ())), preferred_element_type=jnp.float32
        )
        gate = jax.nn.sigmoid(pre)
        out_all[:, :, columns] = (pre * gate).astype(jnp.bfloat16).reshape(f, width, step)
        cot = cot_all[:, :, columns].reshape(full, step).astype(jnp.float32)
        grad = (cot * gate * (1.0 + pre * (1.0 - gate))).astype(jnp.bfloat16)
        back = jnp.dot(weight[...], grad, preferred_element_type=jnp.float32)
        grad_agg[:, columns] = back
        scaled[:, columns] = (back * inv_root[:, columns]).astype(jnp.bfloat16)
        w_terms[...] += lax.dot_general(
            agg[:, columns], grad, (((1,), (1,)), ((), ())), preferred_element_type=jnp.float32
        )

    out[...] = out_all[feat[0]]
    tiles, block, _ = masks_bf.shape
    owners = acc.shape[0]

    @pl.loop(0, owners)
    def _(o):
        acc[o] = jnp.zeros_like(acc[o])

    def tile(t, carry):
        taken = scaled[:, pl.ds(pl.multiple_of(rows[t] * block, block), block)]
        columns = pl.ds(pl.multiple_of(sub[t] * block, block), block)
        acc[owner[t], :, columns] += jnp.dot(
            taken, masks_bf[t], preferred_element_type=jnp.float32
        )
        return carry

    lax.fori_loop(0, tiles, tile, 0, unroll=8)

    @pl.loop(0, owners)
    def _(o):
        part[o] = acc[o].astype(jnp.bfloat16)


def reduce_kernel(
    n, part, w_terms, total, w_total,
    x_buf, z_out, z_buf, w_sum, w_buf, sems, w_send, w_recv,
):
    me, low, partner, ahead, behind = places("dom", n)
    half = n // 2
    greet(mates("dom", n), [])
    order = list(range(1, half)) + [0]
    rows = part.shape[1] // PIECES
    spans = [pl.ds(p * rows, rows) for p in range(PIECES)]
    steps = [(p, k) for p in range(PIECES) for k in order]
    x_copies = {
        (p, k): send(
            part.at[ahead[k] * 2 + 1 - low, spans[p]], x_buf.at[k, spans[p]],
            sems.at[0, k, p], sems.at[1, k, p], dom=partner,
        )
        for p, k in steps
    }
    z_copies = {
        (p, k): send(
            z_out.at[k, spans[p]], z_buf.at[k, spans[p]],
            sems.at[2, k, p], sems.at[3, k, p], dom=ahead[k] * 2 + low,
        )
        for p, k in steps
        if k
    }
    rounds = n.bit_length() - 1
    w_copies = []
    for b in range(rounds):
        bit = lax.rem(me // (1 << b), 2)
        mate = me + (1 - 2 * bit) * (1 << b)
        src = w_terms if b == 0 else w_sum.at[b - 1]
        w_copies.append(send(src, w_buf.at[b], w_send.at[b], w_recv.at[b], dom=mate))
    for k in order:
        x_copies[0, k].start()
    w_copies[0].start()
    for p, k in steps[half:]:
        x_copies[p, k].start()

    def w_round(b):
        w_copies[b].wait_recv()
        held = w_terms[...] if b == 0 else w_sum[b - 1]
        summed = held + w_buf[b]
        if b == rounds - 1:
            w_total[...] = summed
        else:
            w_sum[b] = summed
            w_copies[b + 1].start()

    for i, (p, k) in enumerate(steps):
        if i % half == 0 and 0 < i // half <= rounds:
            w_round(i // half - 1)
        x_copies[p, k].wait_recv()
        span = spans[p]
        value = x_buf[k, span].astype(jnp.float32) + part[ahead[k] * 2 + low, span].astype(
            jnp.float32
        )
        if k:
            z_out[k, span] = value.astype(jnp.bfloat16)
            z_copies[p, k].start()
        else:
            total[span] = value
    for b in range(PIECES - 1, rounds):
        w_round(b)
    for p in range(PIECES):
        span = spans[p]
        value = total[span]
        for k in range(1, half):
            z_copies[p, k].wait_recv()
            value += z_buf[k, span].astype(jnp.float32)
        total[span] = value
    for copy in list(x_copies.values()) + list(z_copies.values()) + w_copies:
        copy.wait_send()


def finish_kernel(scale, total, grad_agg, w_total, embed_grad, weight_grad):
    embed_grad[...] = grad_agg[...] + total[...]
    weight_grad[...] = w_total[...] * scale


def params(collective_id=None):
    if collective_id is None:
        return pltpu.CompilerParams(vmem_limit_bytes=VMEM_LIMIT)
    return pltpu.CompilerParams(
        collective_id=collective_id, has_side_effects=True, vmem_limit_bytes=VMEM_LIMIT
    )


def per_device(embed, weight, cotangent, edge_masks, tile_rows, tile_owner, tile_sub):
    width, local_nodes = embed.shape
    tiles, block, _ = edge_masks.shape
    blocks = local_nodes // block
    n = lax.axis_size("dom")
    f = lax.axis_size("feat")
    full = f * width
    half = n // 2
    rounds = n.bit_length() - 1
    bf, f32 = jnp.bfloat16, jnp.float32
    dma = pltpu.SemaphoreType.DMA
    owner = tile_owner.reshape(tiles)

    gath, cot_all, w_all, masks_bf = pl.pallas_call(
        functools.partial(gather_kernel, n, f),
        out_shape=(
            jax.ShapeDtypeStruct((n, width, local_nodes), bf),
            jax.ShapeDtypeStruct((f, width, local_nodes), bf),
            jax.ShapeDtypeStruct((f, width, full), bf),
            jax.ShapeDtypeStruct((tiles, block, block), bf),
        ),
        in_specs=[VMEM, VMEM, VMEM, ANY],
        out_specs=(VMEM, VMEM, VMEM, ANY),
        scratch_shapes=[
            pltpu.VMEM((tiles, block, block), jnp.int32),
            pltpu.VMEM((tiles, block, block), bf),
            dma((tiles // CHUNK,)),
            dma((tiles // CHUNK,)),
            dma((4, half, PIECES)),
            dma((4, f // 2, PIECES)),
            dma((4, f // 2, 1)),
        ],
        compiler_params=params(0),
        name="gather",
    )(embed, cotangent, weight, edge_masks)

    agg, inv_root = pl.pallas_call(
        forward_kernel,
        out_shape=(
            jax.ShapeDtypeStruct((width, local_nodes), bf),
            jax.ShapeDtypeStruct((1, local_nodes), f32),
        ),
        in_specs=[SMEM] * 3 + [VMEM] * 3,
        out_specs=(VMEM,) * 2,
        scratch_shapes=[pltpu.VMEM((blocks, width + ONES, block), f32)],
        compiler_params=params(),
        name="forward",
    )(tile_rows, owner, tile_sub, gath, masks_bf, embed)

    agg_all = pl.pallas_call(
        functools.partial(share_kernel, f),
        out_shape=jax.ShapeDtypeStruct((f, width, local_nodes), bf),
        in_specs=[VMEM],
        out_specs=VMEM,
        scratch_shapes=[dma((4, f // 2, PIECES))],
        compiler_params=params(1),
        name="share",
    )(agg)

    output, grad_agg, w_terms, part = pl.pallas_call(
        functools.partial(backward_kernel, f),
        out_shape=(
            jax.ShapeDtypeStruct((width, local_nodes), bf),
            jax.ShapeDtypeStruct((width, local_nodes), f32),
            jax.ShapeDtypeStruct((width, full), f32),
            jax.ShapeDtypeStruct((n, width, local_nodes), bf),
        ),
        in_specs=[SMEM] * 4 + [VMEM] * 7,
        out_specs=(VMEM,) * 4,
        scratch_shapes=[
            pltpu.VMEM((width, local_nodes), bf),
            pltpu.VMEM((f, width, local_nodes), bf),
            pltpu.VMEM((n, width, local_nodes), f32),
        ],
        compiler_params=params(),
        name="backward",
    )(
        tile_rows, owner, tile_sub, lax.axis_index("feat").reshape(1).astype(jnp.int32),
        agg, agg_all, w_all, weight, cot_all, inv_root, masks_bf,
    )

    total, w_total = pl.pallas_call(
        functools.partial(reduce_kernel, n),
        out_shape=(
            jax.ShapeDtypeStruct((width, local_nodes), f32),
            jax.ShapeDtypeStruct((width, full), f32),
        ),
        in_specs=[VMEM] * 2,
        out_specs=(VMEM,) * 2,
        scratch_shapes=[
            pltpu.VMEM((half, width, local_nodes), bf),
            pltpu.VMEM((half, width, local_nodes), bf),
            pltpu.VMEM((half, width, local_nodes), bf),
            pltpu.VMEM((rounds, width, full), f32),
            pltpu.VMEM((rounds, width, full), f32),
            dma((4, half, PIECES)),
            dma((rounds,)),
            dma((rounds,)),
        ],
        compiler_params=params(2),
        name="reduce",
    )(part, w_terms)

    embed_grad, weight_grad = pl.pallas_call(
        functools.partial(finish_kernel, 1.0 / math.sqrt(n * local_nodes)),
        out_shape=(
            jax.ShapeDtypeStruct((width, local_nodes), f32),
            jax.ShapeDtypeStruct((width, full), f32),
        ),
        in_specs=[VMEM] * 3,
        out_specs=(VMEM,) * 2,
        compiler_params=params(),
        name="finish",
    )(total, grad_agg, w_total)
    return (output, embed_grad, weight_grad)


def solution(mesh):
    in_specs = (
        P("feat", "dom"),
        P("feat", None),
        P("feat", "dom"),
        P("dom", None, None),
        P("dom"),
        P("dom", None),
        P("dom"),
    )
    out_specs = (P("feat", "dom"), P("feat", "dom"), P("feat", None))
    return jax.shard_map(
        per_device, mesh=mesh, in_specs=in_specs, out_specs=out_specs, check_vma=False
    )
```

```python
import functools
import math

import jax
import jax.numpy as jnp
from jax import lax
from jax.experimental import pallas as pl
from jax.experimental.pallas import tpu as pltpu
from jax.sharding import PartitionSpec as P

MESH = pl.DeviceIdType.MESH
VMEM = pl.BlockSpec(memory_space=pltpu.VMEM)
ANY = pl.BlockSpec(memory_space=pl.ANY)
ONES = 16
CHUNK = 16
PIECES = 4
VMEM_LIMIT = 56 * 1024 * 1024


def greet(dom_mates, feat_mates):
    barrier = pltpu.get_barrier_semaphore()
    for mate in dom_mates:
        pl.semaphore_signal(barrier, inc=1, device_id={"dom": mate}, device_id_type=MESH)
    for mate in feat_mates:
        pl.semaphore_signal(barrier, inc=1, device_id={"feat": mate}, device_id_type=MESH)
    pl.semaphore_wait(barrier, len(dom_mates) + len(feat_mates))


def send(src, dst, send_sem, recv_sem, **where):
    return pltpu.make_async_remote_copy(
        src_ref=src,
        dst_ref=dst,
        send_sem=send_sem,
        recv_sem=recv_sem,
        device_id=where,
        device_id_type=MESH,
    )


def places(axis, n):
    me = lax.axis_index(axis)
    half = n // 2
    high, low = me // 2, lax.rem(me, 2)
    ahead = [lax.rem(high + k, half) for k in range(half)]
    behind = [lax.rem(high + half - k, half) for k in range(half)]
    return me, low, me + 1 - 2 * low, ahead, behind


def mates(axis, n):
    _, low, partner, ahead, _ = places(axis, n)
    return [ahead[k] * 2 + low for k in range(1, n // 2)] + [partner]


class Gather:
    def __init__(self, axis, n, src, dst, sems, pieces):
        me, low, partner, ahead, behind = places(axis, n)
        half = n // 2
        rows = src.shape[0] // pieces
        self.pieces = pieces
        self.first, self.second, self.own = [], [], []
        spans = [pl.ds(p * rows, rows) for p in range(pieces)]
        for p, part in enumerate(spans):
            self.own.append(
                send(
                    src.at[part], dst.at[me, part], sems.at[2, 0, p], sems.at[3, 0, p],
                    **{axis: partner},
                )
            )
        for k in range(1, half):
            for p, part in enumerate(spans):
                self.first.append(
                    send(
                        src.at[part], dst.at[me, part], sems.at[0, k, p], sems.at[1, k, p],
                        **{axis: ahead[k] * 2 + low},
                    )
                )
                slot = dst.at[behind[k] * 2 + low, part]
                self.second.append(
                    send(slot, slot, sems.at[2, k, p], sems.at[3, k, p], **{axis: partner})
                )
        self.at = 0

    def start(self):
        for p, copy in enumerate(self.own):
            if self.first:
                self.first[p].start()
            copy.start()
        for copy in self.first[self.pieces :]:
            copy.start()

    def forward(self, count):
        for _ in range(count):
            if self.at < len(self.first):
                self.first[self.at].wait_recv()
                self.second[self.at].start()
                self.at += 1

    def forward_all(self):
        self.forward(len(self.first))

    def arrive(self, k):
        copies = self.own if k == 0 else self.second[(k - 1) * self.pieces : k * self.pieces]
        for copy in copies:
            copy.wait_recv()

    def sent(self):
        for copy in self.first + self.own + self.second:
            copy.wait_send()


def columns_of(b, block):
    return pl.ds(pl.multiple_of(b * block, block), block)


def run_tiles(first, last, step, carry):
    count = last - first
    unroll = 8 if count % 8 == 0 else 1
    return lax.fori_loop(first, last, step, carry, unroll=unroll)


F_TILE, F_OWNER, F_SUB, R_POS, B_TILE, B_ROW, R_LAST, B_LAST = range(8)
R_SAME, B_SAME, R_SOME, B_SOME = range(4)


def fill_orders(n, blocks, tiles, index, table, flags):
    _, low, _, _, _ = places("dom", n)
    high = lax.axis_index("dom") // 2
    half = n // 2
    tp = index.shape[1]
    rows, owner, sub = index[0:1, :], index[1:2, :], index[2:3, :]
    lane = lax.broadcasted_iota(jnp.int32, (tp, tp), 1)
    tile_row = lax.broadcasted_iota(jnp.int32, (1, tp), 1)
    valid = tile_row < tiles
    other = jnp.where(lax.rem(owner, 2) == low, 0, 1)
    owner_high = owner // 2
    arrival = lax.rem(high + half - owner_high, half) * 2 + other
    turn = lax.rem(owner_high + 2 * half - 1 - high, half)
    dest = ((1 - other) * half + turn) * blocks + sub

    def down(row):
        return jnp.broadcast_to(row, (tp, tp)).T

    def ranks(group):
        key = jnp.where(valid, group * tp + tile_row, (1 << 30) + tile_row)
        wide = jnp.broadcast_to(key, (tp, tp))
        before = jnp.where(wide < wide.T, 1, 0)
        group = jnp.broadcast_to(group, (tp, tp))
        alike = jnp.where(group == group.T, before, 0)
        place = jnp.sum(before, axis=1, keepdims=True)
        same = jnp.where(jnp.sum(alike, axis=1, keepdims=True) > 0, 1.0, 0.0)
        return place, same

    def put(ref, slot, rank, column):
        picked = jnp.where(rank == lane, column, jnp.zeros_like(column))
        ref[slot : slot + 1, 0:tp] = jnp.sum(picked, axis=0, keepdims=True)

    def ends(last_slot, some_slot, column, bound):
        lanes = lax.broadcasted_iota(jnp.int32, (tp, bound), 1)
        column = column[:, 0:1]
        upto = jnp.sum(jnp.where(column <= lanes, 1, 0), axis=0, keepdims=True)
        some = jnp.sum(jnp.where(column == lanes, 1, 0), axis=0, keepdims=True)
        table[last_slot : last_slot + 1, 0:bound] = jnp.maximum(upto - 1, 0)
        flags[some_slot : some_slot + 1, 0:bound] = jnp.where(some > 0, 1.0, 0.0)

    table[...] = jnp.zeros_like(table)
    flags[...] = jnp.zeros_like(flags)
    tile_col = down(tile_row)
    row_col = down(jnp.where(valid, rows, 1 << 20))
    dest_col = down(jnp.where(valid, dest, 1 << 20))
    by_arrival, _ = ranks(arrival)
    put(table, F_TILE, by_arrival, tile_col)
    put(table, F_OWNER, by_arrival, down(owner))
    put(table, F_SUB, by_arrival, down(sub))
    by_row, same_row = ranks(rows)
    put(table, R_POS, by_row, by_arrival)
    put(flags, R_SAME, by_row, same_row)
    by_dest, same_dest = ranks(dest)
    put(table, B_TILE, by_dest, tile_col)
    put(table, B_ROW, by_dest, down(rows))
    put(flags, B_SAME, by_dest, same_dest)
    ends(R_LAST, R_SOME, row_col, tp)
    ends(B_LAST, B_SOME, dest_col, table.shape[1])


def layer_kernel(
    n, f, embed, cot, weight, masks, index, out, total, w_total,
    gath, ready, cot_all, w_all, agg, agg_all, out_all, scaled, inv_root, grad_agg, raw, narrow,
    own, table, flags, order, marks, f_parts, f_sums, b_sums, x_buf, z_buf, w_sum, w_buf,
    raw_sem, table_sem, e_sems, c_sems, w_sems, a_sems, r_sems, w_send, w_recv,
):
    me, low, partner, ahead, behind = places("dom", n)
    feat = lax.axis_index("feat")
    half = n // 2
    tiles, block, _ = masks.shape
    width, local_nodes = embed.shape
    blocks = local_nodes // block
    full = f * width
    cap = -(-2 * tiles // n)
    pieces = tiles // CHUNK
    spans = [pl.ds(c * CHUNK, CHUNK) for c in range(pieces)]
    loads = [
        pltpu.make_async_copy(masks.at[s], raw.at[s], raw_sem.at[c]) for c, s in enumerate(spans)
    ]
    for load in loads:
        load.start()
    greet(mates("dom", n), mates("feat", f))
    for b in range(blocks):
        own[b] = embed[:, b * block : (b + 1) * block]
    e_gather = Gather("dom", n, own, gath, e_sems, PIECES)
    c_gather = Gather("feat", f, cot, cot_all, c_sems, PIECES)
    w_gather = Gather("feat", f, weight, w_all, w_sems, 1)
    for gather in (e_gather, w_gather, c_gather):
        gather.start()
    ready[me] = own[...]
    cot_all[feat] = cot[...]
    w_all[feat] = weight[...]
    fill_orders(n, blocks, tiles, index, table, flags)
    to_scalars = [
        pltpu.make_async_copy(table, order, table_sem.at[0]),
        pltpu.make_async_copy(flags, marks, table_sem.at[1]),
    ]
    for copy in to_scalars:
        copy.start()
    for c in range(pieces):
        loads[c].wait()

        @pl.loop(c * CHUNK, (c + 1) * CHUNK)
        def _(t):
            narrow[t] = raw[t].astype(jnp.float32).astype(jnp.bfloat16)

        e_gather.forward(1)
    w_gather.forward_all()
    e_gather.forward_all()
    c_gather.forward_all()
    for copy in to_scalars:
        copy.wait()

    for k in range(1, half):
        ready[behind[k] * 2 + low] = gath[behind[k] * 2 + low]
    ones = jnp.ones((ONES, block), jnp.bfloat16)

    def forward_tile(k, carry):
        taken = ready[order[F_OWNER, k], order[F_SUB, k]]
        f_parts[k] = lax.dot_general(
            jnp.concatenate([taken, ones], axis=0),
            narrow[order[F_TILE, k]],
            (((1,), (1,)), ((), ())),
            preferred_element_type=jnp.float32,
        )
        return carry

    at = 0
    for rank in range(n):
        begin = max(0, tiles - cap * (n - rank))
        if rank % 2:
            if begin > at:
                run_tiles(at, begin, forward_tile, 0)
                at = begin
            e_gather.arrive(rank // 2)
            source = behind[rank // 2] * 2 + 1 - low
            ready[source] = gath[source]
    run_tiles(at, tiles, forward_tile, 0)

    def add_row(k, held):
        held = held * marks[R_SAME, k] + f_parts[order[R_POS, k]]
        f_sums[k] = held
        return held

    run_tiles(0, tiles, add_row, jnp.zeros((width + ONES, block), jnp.float32))

    def segment(sums, last, some, b):
        return sums[order[last, b]] * marks[some, b]

    for b in range(blocks):
        columns = slice(b * block, (b + 1) * block)
        value = segment(f_sums, R_LAST, R_SOME, b)
        root = 1.0 / jnp.sqrt(1.0 + value[width : width + 1, :])
        inv_root[:, columns] = root
        agg[:, columns] = (
            embed[:, columns].astype(jnp.float32) + value[:width, :] * root
        ).astype(jnp.bfloat16)

    a_gather = Gather("feat", f, agg, agg_all, a_sems, PIECES)
    a_gather.start()
    agg_all[feat] = agg[...]
    for k in range(f // 2):
        w_gather.arrive(k)
        c_gather.arrive(k)
    whole_w = w_all[...].reshape(full, full)
    w_total[...] = jnp.zeros_like(w_total)
    a_gather.forward_all()
    for k in range(f // 2):
        a_gather.arrive(k)
    step = 2 * block

    @pl.loop(0, local_nodes // step)
    def _(c):
        columns = columns_of(c, step)
        values = agg_all[:, :, columns].reshape(full, step)
        pre = lax.dot_general(
            whole_w, values, (((0,), (0,)), ((), ())), preferred_element_type=jnp.float32
        )
        gate = jax.nn.sigmoid(pre)
        out_all[:, :, columns] = (pre * gate).astype(jnp.bfloat16).reshape(f, width, step)
        given = cot_all[:, :, columns].reshape(full, step).astype(jnp.float32)
        grad = (given * gate * (1.0 + pre * (1.0 - gate))).astype(jnp.bfloat16)
        back = jnp.dot(weight[...], grad, preferred_element_type=jnp.float32)
        grad_agg[:, columns] = back
        narrowed = (back * inv_root[:, columns]).astype(jnp.bfloat16)
        for b in range(step // block):
            scaled[c * (step // block) + b] = narrowed[:, b * block : (b + 1) * block]
        w_total[...] += lax.dot_general(
            agg[:, columns], grad, (((1,), (1,)), ((), ())), preferred_element_type=jnp.float32
        )

    rounds = n.bit_length() - 1
    w_copies = []
    for b in range(rounds):
        bit = lax.rem(me // (1 << b), 2)
        mate = me + (1 - 2 * bit) * (1 << b)
        w_copies.append(send(w_sum.at[b], w_buf.at[b], w_send.at[b], w_recv.at[b], dom=mate))
    w_sum[0] = w_total[...]
    w_copies[0].start()

    def w_round(b):
        w_copies[b].wait_recv()
        summed = w_sum[b] + w_buf[b]
        if b == rounds - 1:
            w_total[...] = summed * (1.0 / math.sqrt(n * local_nodes))
        else:
            w_sum[b + 1] = summed
            w_copies[b + 1].start()

    turns = list(range(1, half)) + [0]
    group = blocks // PIECES
    parts = [pl.ds(p * group, group) for p in range(PIECES)]
    x_out, z_out = ready.at[pl.ds(0, half)], ready.at[pl.ds(half, half)]
    x_copies = {
        (k, p): send(
            x_out.at[k, part], x_buf.at[k, part], r_sems.at[0, k, p], r_sems.at[1, k, p],
            dom=partner,
        )
        for k in turns
        for p, part in enumerate(parts)
    }
    z_copies = {
        (k, p): send(
            z_out.at[k, part], z_buf.at[k, part], r_sems.at[2, k, p], r_sems.at[3, k, p],
            dom=ahead[k] * 2 + low,
        )
        for k in turns[:-1]
        for p, part in enumerate(parts)
    }

    def backward_tile(k, held):
        held = held * marks[B_SAME, k] + jnp.dot(
            scaled[order[B_ROW, k]],
            narrow[order[B_TILE, k]],
            preferred_element_type=jnp.float32,
        )
        b_sums[k] = held
        return held

    held = jnp.zeros((width, block), jnp.float32)
    at = 0
    for j, k in enumerate(turns):
        upto = min(tiles, cap * (j + 1)) if j < half - 1 else tiles
        held = run_tiles(at, upto, backward_tile, held)
        at = upto
        for b in range(blocks):
            value = segment(b_sums, B_LAST, B_SOME, j * blocks + b)
            x_out[k, b] = value.astype(jnp.bfloat16)
        for p in range(PIECES):
            x_copies[k, p].start()
    for j, k in enumerate(turns):
        for b in range(blocks):
            columns = slice(b * block, (b + 1) * block)
            value = segment(b_sums, B_LAST, B_SOME, (half + j) * blocks + b)
            if k:
                z_out[k, b] = value.astype(jnp.bfloat16)
            else:
                total[:, columns] = grad_agg[:, columns] + value
    for j, k in enumerate(turns):
        for p, part in enumerate(parts):
            x_copies[k, p].wait_recv()
            for b in range(p * group, (p + 1) * group):
                came = x_buf[k, b].astype(jnp.float32)
                if k:
                    z_out[k, b] = (z_out[k, b].astype(jnp.float32) + came).astype(jnp.bfloat16)
                else:
                    total[:, b * block : (b + 1) * block] += came
            if k:
                z_copies[k, p].start()
        if j < rounds:
            w_round(j)
    for b in range(half, rounds):
        w_round(b)
    for k in turns[:-1]:
        for p, part in enumerate(parts):
            z_copies[k, p].wait_recv()
            for b in range(p * group, (p + 1) * group):
                total[:, b * block : (b + 1) * block] += z_buf[k, b].astype(jnp.float32)
    out[...] = out_all[feat]
    for gather in (e_gather, w_gather, c_gather, a_gather):
        gather.sent()
    for copy in list(x_copies.values()) + list(z_copies.values()) + w_copies:
        copy.wait_send()


def finish_kernel(out, total, w_total, output, embed_grad, weight_grad):
    output[...] = out[...]
    embed_grad[...] = total[...]
    weight_grad[...] = w_total[...]


def params(collective_id=None):
    if collective_id is None:
        return pltpu.CompilerParams(vmem_limit_bytes=VMEM_LIMIT)
    return pltpu.CompilerParams(
        collective_id=collective_id, has_side_effects=True, vmem_limit_bytes=VMEM_LIMIT
    )


def per_device(embed, weight, cotangent, edge_masks, tile_rows, tile_owner, tile_sub):
    width, local_nodes = embed.shape
    tiles, block, _ = edge_masks.shape
    blocks = local_nodes // block
    n = lax.axis_size("dom")
    f = lax.axis_size("feat")
    full = f * width
    half = n // 2
    rounds = n.bit_length() - 1
    bf, f32 = jnp.bfloat16, jnp.float32
    dma = pltpu.SemaphoreType.DMA
    lanes = -(-tiles // 128) * 128
    index = jnp.pad(
        jnp.stack([tile_rows, tile_owner.reshape(tiles), tile_sub]), ((0, 0), (0, lanes - tiles))
    )
    table = (8, max(lanes, -(-n * blocks // 128) * 128))
    shard = (width, local_nodes)

    results = (
        jax.ShapeDtypeStruct(shard, bf),
        jax.ShapeDtypeStruct(shard, f32),
        jax.ShapeDtypeStruct((width, full), f32),
    )
    layer = pl.pallas_call(
        functools.partial(layer_kernel, n, f),
        out_shape=results,
        in_specs=[VMEM, VMEM, VMEM, ANY, VMEM],
        out_specs=(VMEM,) * 3,
        scratch_shapes=[
            pltpu.VMEM((n, blocks, width, block), bf),
            pltpu.VMEM((n, blocks, width, block), bf),
            pltpu.VMEM((f, *shard), bf),
            pltpu.VMEM((f, width, full), bf),
            pltpu.VMEM(shard, bf),
            pltpu.VMEM((f, *shard), bf),
            pltpu.VMEM((f, *shard), bf),
            pltpu.VMEM((blocks, width, block), bf),
            pltpu.VMEM((1, local_nodes), f32),
            pltpu.VMEM(shard, f32),
            pltpu.VMEM((tiles, block, block), jnp.int32),
            pltpu.VMEM((tiles, block, block), bf),
            pltpu.VMEM((blocks, width, block), bf),
            pltpu.VMEM(table, jnp.int32),
            pltpu.VMEM(table, f32),
            pltpu.SMEM(table, jnp.int32),
            pltpu.SMEM(table, f32),
            pltpu.VMEM((tiles, width + ONES, block), f32),
            pltpu.VMEM((tiles, width + ONES, block), f32),
            pltpu.VMEM((tiles, width, block), f32),
            pltpu.VMEM((half, blocks, width, block), bf),
            pltpu.VMEM((half, blocks, width, block), bf),
            pltpu.VMEM((rounds, width, full), f32),
            pltpu.VMEM((rounds, width, full), f32),
            dma((tiles // CHUNK,)),
            dma((2,)),
            dma((4, half, PIECES)),
            dma((4, f // 2, PIECES)),
            dma((4, f // 2, 1)),
            dma((4, f // 2, PIECES)),
            dma((4, half, PIECES)),
            dma((rounds,)),
            dma((rounds,)),
        ],
        compiler_params=params(0),
        name="layer",
    )(embed, cotangent, weight, edge_masks, index)
    output, embed_grad, weight_grad = pl.pallas_call(
        finish_kernel,
        out_shape=results,
        in_specs=[VMEM] * 3,
        out_specs=(VMEM,) * 3,
        compiler_params=params(),
        name="finish",
    )(*layer)
    return (output, embed_grad, weight_grad)


def solution(mesh):
    in_specs = (
        P("feat", "dom"),
        P("feat", None),
        P("feat", "dom"),
        P("dom", None, None),
        P("dom"),
        P("dom", None),
        P("dom"),
    )
    out_specs = (P("feat", "dom"), P("feat", "dom"), P("feat", None))
    return jax.shard_map(
        per_device, mesh=mesh, in_specs=in_specs, out_specs=out_specs, check_vma=False
    )
```

```python
import functools
import math

import jax
import jax.numpy as jnp
from jax import lax
from jax.experimental import pallas as pl
from jax.experimental.pallas import tpu as pltpu
from jax.sharding import PartitionSpec as P

MESH = pl.DeviceIdType.MESH
VMEM = pl.BlockSpec(memory_space=pltpu.VMEM)
ANY = pl.BlockSpec(memory_space=pl.ANY)
ONES = 16
CHUNK = 16
PIECES = 4
VMEM_LIMIT = 56 * 1024 * 1024


def greet(dom_mates, feat_mates):
    barrier = pltpu.get_barrier_semaphore()
    for mate in dom_mates:
        pl.semaphore_signal(barrier, inc=1, device_id={"dom": mate}, device_id_type=MESH)
    for mate in feat_mates:
        pl.semaphore_signal(barrier, inc=1, device_id={"feat": mate}, device_id_type=MESH)
    pl.semaphore_wait(barrier, len(dom_mates) + len(feat_mates))


def send(src, dst, send_sem, recv_sem, **where):
    return pltpu.make_async_remote_copy(
        src_ref=src,
        dst_ref=dst,
        send_sem=send_sem,
        recv_sem=recv_sem,
        device_id=where,
        device_id_type=MESH,
    )


def places(axis, n):
    me = lax.axis_index(axis)
    half = n // 2
    high, low = me // 2, lax.rem(me, 2)
    ahead = [lax.rem(high + k, half) for k in range(half)]
    behind = [lax.rem(high + half - k, half) for k in range(half)]
    return me, low, me + 1 - 2 * low, ahead, behind


def mates(axis, n):
    _, low, partner, ahead, _ = places(axis, n)
    return [ahead[k] * 2 + low for k in range(1, n // 2)] + [partner]


class Gather:
    def __init__(self, axis, n, src, dst, sems, pieces):
        me, low, partner, ahead, behind = places(axis, n)
        half = n // 2
        rows = src.shape[0] // pieces
        self.pieces = pieces
        self.first, self.second, self.own = [], [], []
        spans = [pl.ds(p * rows, rows) for p in range(pieces)]
        for p, part in enumerate(spans):
            self.own.append(
                send(
                    src.at[part], dst.at[me, part], sems.at[2, 0, p], sems.at[3, 0, p],
                    **{axis: partner},
                )
            )
        for k in range(1, half):
            for p, part in enumerate(spans):
                self.first.append(
                    send(
                        src.at[part], dst.at[me, part], sems.at[0, k, p], sems.at[1, k, p],
                        **{axis: ahead[k] * 2 + low},
                    )
                )
                slot = dst.at[behind[k] * 2 + low, part]
                self.second.append(
                    send(slot, slot, sems.at[2, k, p], sems.at[3, k, p], **{axis: partner})
                )
        self.at = 0

    def start(self):
        for p, copy in enumerate(self.own):
            if self.first:
                self.first[p].start()
            copy.start()
        for copy in self.first[self.pieces :]:
            copy.start()

    def start_piece(self, p):
        for copy in self.first[p :: self.pieces] + [self.own[p]]:
            copy.start()

    def forward_piece(self, p):
        for came, on in zip(self.first[p :: self.pieces], self.second[p :: self.pieces]):
            came.wait_recv()
            on.start()

    def arrive_piece(self, p):
        for copy in [self.own[p]] + self.second[p :: self.pieces]:
            copy.wait_recv()

    def forward(self, count):
        for _ in range(count):
            if self.at < len(self.first):
                self.first[self.at].wait_recv()
                self.second[self.at].start()
                self.at += 1

    def forward_all(self):
        self.forward(len(self.first))

    def arrive(self, k):
        copies = self.own if k == 0 else self.second[(k - 1) * self.pieces : k * self.pieces]
        for copy in copies:
            copy.wait_recv()

    def sent(self):
        for copy in self.first + self.own + self.second:
            copy.wait_send()


def run_tiles(first, last, step, carry):
    count = last - first
    unroll = 8 if count % 8 == 0 else 1
    return lax.fori_loop(first, last, step, carry, unroll=unroll)


F_TILE, F_OWNER, F_SUB, R_POS, B_TILE, B_ROW, R_LAST, B_LAST = range(8)
R_SAME, B_SAME, R_SOME, B_SOME = range(4)


def fill_orders(n, blocks, rows_in, owner_in, sub_in, pad, table, flags):
    _, low, _, _, _ = places("dom", n)
    high = lax.axis_index("dom") // 2
    half = n // 2
    tp = pad.shape[1]
    tiles = owner_in.shape[1]
    pad[...] = jnp.zeros_like(pad)
    pad[0:1, 0:tiles] = rows_in[...]
    pad[1:2, 0:tiles] = owner_in[...]
    pad[2:3, 0:tiles] = sub_in[...]
    rows, owner, sub = pad[0:1, :], pad[1:2, :], pad[2:3, :]
    lane = lax.broadcasted_iota(jnp.int32, (tp, tp), 1)
    tile_row = lax.broadcasted_iota(jnp.int32, (1, tp), 1)
    valid = tile_row < tiles
    other = jnp.where(lax.rem(owner, 2) == low, 0, 1)
    owner_high = owner // 2
    arrival = lax.rem(high + half - owner_high, half) * 2 + other
    turn = lax.rem(owner_high + 2 * half - 1 - high, half)
    dest = ((1 - other) * half + turn) * blocks + sub

    def down(row):
        return jnp.broadcast_to(row, (tp, tp)).T

    def ranks(group):
        key = jnp.where(valid, group * tp + tile_row, (1 << 30) + tile_row)
        wide = jnp.broadcast_to(key, (tp, tp))
        before = jnp.where(wide < wide.T, 1, 0)
        group = jnp.broadcast_to(group, (tp, tp))
        alike = jnp.where(group == group.T, before, 0)
        place = jnp.sum(before, axis=1, keepdims=True)
        same = jnp.where(jnp.sum(alike, axis=1, keepdims=True) > 0, 1.0, 0.0)
        return place, same

    def put(ref, slot, rank, column):
        picked = jnp.where(rank == lane, column, jnp.zeros_like(column))
        ref[slot : slot + 1, 0:tp] = jnp.sum(picked, axis=0, keepdims=True)

    def ends(last_slot, some_slot, column, bound):
        lanes = lax.broadcasted_iota(jnp.int32, (tp, bound), 1)
        column = column[:, 0:1]
        upto = jnp.sum(jnp.where(column <= lanes, 1, 0), axis=0, keepdims=True)
        some = jnp.sum(jnp.where(column == lanes, 1, 0), axis=0, keepdims=True)
        table[last_slot : last_slot + 1, 0:bound] = jnp.maximum(upto - 1, 0)
        flags[some_slot : some_slot + 1, 0:bound] = jnp.where(some > 0, 1.0, 0.0)

    table[...] = jnp.zeros_like(table)
    flags[...] = jnp.zeros_like(flags)
    tile_col = down(tile_row)
    row_col = down(jnp.where(valid, rows, 1 << 20))
    dest_col = down(jnp.where(valid, dest, 1 << 20))
    by_arrival, _ = ranks(arrival)
    put(table, F_TILE, by_arrival, tile_col)
    put(table, F_OWNER, by_arrival, down(owner))
    put(table, F_SUB, by_arrival, down(sub))
    by_row, same_row = ranks(rows)
    put(table, R_POS, by_row, by_arrival)
    put(flags, R_SAME, by_row, same_row)
    by_dest, same_dest = ranks(dest)
    put(table, B_TILE, by_dest, tile_col)
    put(table, B_ROW, by_dest, down(rows))
    put(flags, B_SAME, by_dest, same_dest)
    ends(R_LAST, R_SOME, row_col, tp)
    ends(B_LAST, B_SOME, dest_col, table.shape[1])


def layer_kernel(
    n, f, embed, cot, weight, masks, rows_in, owner_in, sub_in, out, total, w_total,
    gath, ready, cot_all, w_all, agg, agg_all, out_all, scaled, inv_root, grad_agg, raw, narrow,
    own, pad, table, flags, order, marks, f_parts, f_sums, b_sums, x_buf, z_buf, w_sum, w_buf,
    raw_sem, table_sem, e_sems, c_sems, w_sems, a_sems, r_sems, w_send, w_recv,
):
    me, low, partner, ahead, behind = places("dom", n)
    feat = lax.axis_index("feat")
    half = n // 2
    tiles, block, _ = masks.shape
    width, local_nodes = embed.shape
    blocks = local_nodes // block
    full = f * width
    cap = -(-2 * tiles // n)
    pieces = tiles // CHUNK
    spans = [pl.ds(c * CHUNK, CHUNK) for c in range(pieces)]
    loads = [
        pltpu.make_async_copy(masks.at[s], raw.at[s], raw_sem.at[c]) for c, s in enumerate(spans)
    ]
    for load in loads:
        load.start()
    greet(mates("dom", n), mates("feat", f))
    for b in range(blocks):
        own[b] = embed[:, b * block : (b + 1) * block]
    e_gather = Gather("dom", n, own, gath, e_sems, PIECES)
    c_gather = Gather("feat", f, cot, cot_all, c_sems, PIECES)
    w_gather = Gather("feat", f, weight, w_all, w_sems, 1)
    for gather in (e_gather, w_gather, c_gather):
        gather.start()
    ready[me] = own[...]
    cot_all[feat] = cot[...]
    w_all[feat] = weight[...]
    fill_orders(n, blocks, rows_in, owner_in, sub_in, pad, table, flags)
    to_scalars = [
        pltpu.make_async_copy(table, order, table_sem.at[0]),
        pltpu.make_async_copy(flags, marks, table_sem.at[1]),
    ]
    for copy in to_scalars:
        copy.start()
    for c in range(pieces):
        loads[c].wait()

        @pl.loop(c * CHUNK, (c + 1) * CHUNK)
        def _(t):
            narrow[t] = raw[t].astype(jnp.float32).astype(jnp.bfloat16)

        e_gather.forward(1)
    w_gather.forward_all()
    e_gather.forward_all()
    c_gather.forward_all()
    for copy in to_scalars:
        copy.wait()

    for k in range(1, half):
        ready[behind[k] * 2 + low] = gath[behind[k] * 2 + low]
    ones = jnp.ones((ONES, block), jnp.bfloat16)

    def forward_tile(k, carry):
        taken = ready[order[F_OWNER, k], order[F_SUB, k]]
        f_parts[k] = lax.dot_general(
            jnp.concatenate([taken, ones], axis=0),
            narrow[order[F_TILE, k]],
            (((1,), (1,)), ((), ())),
            preferred_element_type=jnp.float32,
        )
        return carry

    at = 0
    for rank in range(n):
        begin = max(0, tiles - cap * (n - rank))
        if rank % 2:
            if begin > at:
                run_tiles(at, begin, forward_tile, 0)
                at = begin
            e_gather.arrive(rank // 2)
            source = behind[rank // 2] * 2 + 1 - low
            ready[source] = gath[source]
    run_tiles(at, tiles, forward_tile, 0)

    def add_row(k, held):
        held = held * marks[R_SAME, k] + f_parts[order[R_POS, k]]
        f_sums[k] = held
        return held

    run_tiles(0, tiles, add_row, jnp.zeros((width + ONES, block), jnp.float32))

    def segment(sums, last, some, b):
        return sums[order[last, b]] * marks[some, b]

    a_gather = Gather("feat", f, agg, agg_all, a_sems, PIECES)
    group = blocks // PIECES
    step = group * block
    for b in range(blocks):
        columns = slice(b * block, (b + 1) * block)
        value = segment(f_sums, R_LAST, R_SOME, b)
        root = 1.0 / jnp.sqrt(1.0 + value[width : width + 1, :])
        inv_root[:, columns] = root
        agg[b] = (embed[:, columns].astype(jnp.float32) + value[:width, :] * root).astype(
            jnp.bfloat16
        )
        if (b + 1) % group == 0:
            a_gather.start_piece(b // group)
    agg_all[feat] = agg[...]
    for k in range(f // 2):
        w_gather.arrive(k)
        c_gather.arrive(k)
    whole_w = w_all[...].reshape(full, full)

    def dense(p):
        columns = slice(p * step, (p + 1) * step)
        held = range(p * group, (p + 1) * group)
        values = jnp.concatenate([agg_all[:, b].reshape(full, block) for b in held], axis=1)
        pre = lax.dot_general(
            whole_w, values, (((0,), (0,)), ((), ())), preferred_element_type=jnp.float32
        )
        gate = jax.nn.sigmoid(pre)
        out_all[:, :, columns] = (pre * gate).astype(jnp.bfloat16).reshape(f, width, step)
        given = cot_all[:, :, columns].reshape(full, step).astype(jnp.float32)
        grad = (given * gate * (1.0 + pre * (1.0 - gate))).astype(jnp.bfloat16)
        back = jnp.dot(weight[...], grad, preferred_element_type=jnp.float32)
        grad_agg[:, columns] = back
        narrowed = (back * inv_root[:, columns]).astype(jnp.bfloat16)
        for i, b in enumerate(held):
            scaled[b] = narrowed[:, i * block : (i + 1) * block]
        terms = lax.dot_general(
            jnp.concatenate([agg[b] for b in held], axis=1),
            grad,
            (((1,), (1,)), ((), ())),
            preferred_element_type=jnp.float32,
        )
        if p:
            w_sum[0] += terms
        else:
            w_sum[0] = terms

    a_gather.forward_piece(0)
    for p in range(PIECES):
        if p + 1 < PIECES:
            a_gather.forward_piece(p + 1)
        a_gather.arrive_piece(p)
        dense(p)

    rounds = n.bit_length() - 1
    w_copies = []
    for b in range(rounds):
        bit = lax.rem(me // (1 << b), 2)
        mate = me + (1 - 2 * bit) * (1 << b)
        w_copies.append(send(w_sum.at[b], w_buf.at[b], w_send.at[b], w_recv.at[b], dom=mate))
    w_copies[0].start()

    def w_round(b):
        w_copies[b].wait_recv()
        summed = w_sum[b] + w_buf[b]
        if b == rounds - 1:
            w_total[...] = summed * (1.0 / math.sqrt(n * local_nodes))
        else:
            w_sum[b + 1] = summed
            w_copies[b + 1].start()

    turns = list(range(1, half)) + [0]
    parts = [pl.ds(p * group, group) for p in range(PIECES)]
    x_out, z_out = ready.at[pl.ds(0, half)], ready.at[pl.ds(half, half)]
    x_copies = {
        (k, p): send(
            x_out.at[k, part], x_buf.at[k, part], r_sems.at[0, k, p], r_sems.at[1, k, p],
            dom=partner,
        )
        for k in turns
        for p, part in enumerate(parts)
    }
    z_copies = {
        (k, p): send(
            z_out.at[k, part], z_buf.at[k, part], r_sems.at[2, k, p], r_sems.at[3, k, p],
            dom=ahead[k] * 2 + low,
        )
        for k in turns[:-1]
        for p, part in enumerate(parts)
    }

    def backward_tile(k, held):
        held = held * marks[B_SAME, k] + jnp.dot(
            scaled[order[B_ROW, k]],
            narrow[order[B_TILE, k]],
            preferred_element_type=jnp.float32,
        )
        b_sums[k] = held
        return held

    held = jnp.zeros((width, block), jnp.float32)
    at = 0
    for j, k in enumerate(turns):
        upto = min(tiles, cap * (j + 1)) if j < half - 1 else tiles
        held = run_tiles(at, upto, backward_tile, held)
        at = upto
        for b in range(blocks):
            value = segment(b_sums, B_LAST, B_SOME, j * blocks + b)
            x_out[k, b] = value.astype(jnp.bfloat16)
        for p in range(PIECES):
            x_copies[k, p].start()
    for j, k in enumerate(turns):
        for b in range(blocks):
            columns = slice(b * block, (b + 1) * block)
            value = segment(b_sums, B_LAST, B_SOME, (half + j) * blocks + b)
            if k:
                z_out[k, b] = value.astype(jnp.bfloat16)
            else:
                total[:, columns] = grad_agg[:, columns] + value
    out[...] = out_all[feat]
    for j, k in enumerate(turns):
        for p, part in enumerate(parts):
            x_copies[k, p].wait_recv()
            for b in range(p * group, (p + 1) * group):
                came = x_buf[k, b].astype(jnp.float32)
                if k:
                    z_out[k, b] = (z_out[k, b].astype(jnp.float32) + came).astype(jnp.bfloat16)
                else:
                    total[:, b * block : (b + 1) * block] += came
            if k:
                z_copies[k, p].start()
        if j < rounds:
            w_round(j)
    for b in range(half, rounds):
        w_round(b)
    for k in turns[:-1]:
        for p, part in enumerate(parts):
            z_copies[k, p].wait_recv()
            for b in range(p * group, (p + 1) * group):
                total[:, b * block : (b + 1) * block] += z_buf[k, b].astype(jnp.float32)
    for gather in (e_gather, w_gather, c_gather, a_gather):
        gather.sent()
    for copy in list(x_copies.values()) + list(z_copies.values()) + w_copies:
        copy.wait_send()


def finish_kernel(out, total, w_total, output, embed_grad, weight_grad):
    output[...] = out[...]
    embed_grad[...] = total[...]
    weight_grad[...] = w_total[...]


def params(collective_id=None):
    if collective_id is None:
        return pltpu.CompilerParams(vmem_limit_bytes=VMEM_LIMIT)
    return pltpu.CompilerParams(
        collective_id=collective_id, has_side_effects=True, vmem_limit_bytes=VMEM_LIMIT
    )


def per_device(embed, weight, cotangent, edge_masks, tile_rows, tile_owner, tile_sub):
    width, local_nodes = embed.shape
    tiles, block, _ = edge_masks.shape
    blocks = local_nodes // block
    n = lax.axis_size("dom")
    f = lax.axis_size("feat")
    full = f * width
    half = n // 2
    rounds = n.bit_length() - 1
    bf, f32 = jnp.bfloat16, jnp.float32
    dma = pltpu.SemaphoreType.DMA
    lanes = -(-tiles // 128) * 128
    table = (8, max(lanes, -(-n * blocks // 128) * 128))
    shard = (width, local_nodes)

    results = (
        jax.ShapeDtypeStruct(shard, bf),
        jax.ShapeDtypeStruct(shard, f32),
        jax.ShapeDtypeStruct((width, full), f32),
    )
    layer = pl.pallas_call(
        functools.partial(layer_kernel, n, f),
        out_shape=results,
        in_specs=[VMEM, VMEM, VMEM, ANY, VMEM, VMEM, VMEM],
        out_specs=(VMEM,) * 3,
        scratch_shapes=[
            pltpu.VMEM((n, blocks, width, block), bf),
            pltpu.VMEM((n, blocks, width, block), bf),
            pltpu.VMEM((f, *shard), bf),
            pltpu.VMEM((f, width, full), bf),
            pltpu.VMEM((blocks, width, block), bf),
            pltpu.VMEM((f, blocks, width, block), bf),
            pltpu.VMEM((f, *shard), bf),
            pltpu.VMEM((blocks, width, block), bf),
            pltpu.VMEM((1, local_nodes), f32),
            pltpu.VMEM(shard, f32),
            pltpu.VMEM((tiles, block, block), jnp.int32),
            pltpu.VMEM((tiles, block, block), bf),
            pltpu.VMEM((blocks, width, block), bf),
            pltpu.VMEM((8, lanes), jnp.int32),
            pltpu.VMEM(table, jnp.int32),
            pltpu.VMEM(table, f32),
            pltpu.SMEM(table, jnp.int32),
            pltpu.SMEM(table, f32),
            pltpu.VMEM((tiles, width + ONES, block), f32),
            pltpu.VMEM((tiles, width + ONES, block), f32),
            pltpu.VMEM((tiles, width, block), f32),
            pltpu.VMEM((half, blocks, width, block), bf),
            pltpu.VMEM((half, blocks, width, block), bf),
            pltpu.VMEM((rounds, width, full), f32),
            pltpu.VMEM((rounds, width, full), f32),
            dma((tiles // CHUNK,)),
            dma((2,)),
            dma((4, half, PIECES)),
            dma((4, f // 2, PIECES)),
            dma((4, f // 2, 1)),
            dma((4, f // 2, PIECES)),
            dma((4, half, PIECES)),
            dma((rounds,)),
            dma((rounds,)),
        ],
        compiler_params=params(0),
        name="layer",
    )(
        embed, cotangent, weight, edge_masks,
        tile_rows.reshape(1, tiles), tile_owner.reshape(1, tiles), tile_sub.reshape(1, tiles),
    )
    output, embed_grad, weight_grad = pl.pallas_call(
        finish_kernel,
        out_shape=results,
        in_specs=[VMEM] * 3,
        out_specs=(VMEM,) * 3,
        compiler_params=params(),
        name="finish",
    )(*layer)
    return (output, embed_grad, weight_grad)


def solution(mesh):
    in_specs = (
        P("feat", "dom"),
        P("feat", None),
        P("feat", "dom"),
        P("dom", None, None),
        P("dom"),
        P("dom", None),
        P("dom"),
    )
    out_specs = (P("feat", "dom"), P("feat", "dom"), P("feat", None))
    return jax.shard_map(
        per_device, mesh=mesh, in_specs=in_specs, out_specs=out_specs, check_vma=False
    )
```

```python
import functools
import math

import jax
import jax.numpy as jnp
from jax import lax
from jax.experimental import pallas as pl
from jax.experimental.pallas import tpu as pltpu
from jax.sharding import PartitionSpec as P

MESH = pl.DeviceIdType.MESH
VMEM = pl.BlockSpec(memory_space=pltpu.VMEM)
ANY = pl.BlockSpec(memory_space=pl.ANY)
ONES = 16
CHUNK = 16
PIECES = 4
VMEM_LIMIT = 56 * 1024 * 1024


def greet(dom_mates, feat_mates):
    barrier = pltpu.get_barrier_semaphore()
    for mate in dom_mates:
        pl.semaphore_signal(barrier, inc=1, device_id={"dom": mate}, device_id_type=MESH)
    for mate in feat_mates:
        pl.semaphore_signal(barrier, inc=1, device_id={"feat": mate}, device_id_type=MESH)
    pl.semaphore_wait(barrier, len(dom_mates) + len(feat_mates))


def send(src, dst, send_sem, recv_sem, **where):
    return pltpu.make_async_remote_copy(
        src_ref=src,
        dst_ref=dst,
        send_sem=send_sem,
        recv_sem=recv_sem,
        device_id=where,
        device_id_type=MESH,
    )


def places(axis, n):
    me = lax.axis_index(axis)
    half = n // 2
    high, low = me // 2, lax.rem(me, 2)
    ahead = [lax.rem(high + k, half) for k in range(half)]
    behind = [lax.rem(high + half - k, half) for k in range(half)]
    return me, low, me + 1 - 2 * low, ahead, behind


def mates(axis, n):
    _, low, partner, ahead, _ = places(axis, n)
    return [ahead[k] * 2 + low for k in range(1, n // 2)] + [partner]


class Gather:
    def __init__(self, axis, n, src, dst, sems, pieces):
        me, low, partner, ahead, behind = places(axis, n)
        half = n // 2
        rows = src.shape[0] // pieces
        self.pieces = pieces
        self.first, self.second, self.own = [], [], []
        spans = [pl.ds(p * rows, rows) for p in range(pieces)]
        for p, part in enumerate(spans):
            self.own.append(
                send(
                    src.at[part], dst.at[me, part], sems.at[2, 0, p], sems.at[3, 0, p],
                    **{axis: partner},
                )
            )
        for k in range(1, half):
            for p, part in enumerate(spans):
                self.first.append(
                    send(
                        src.at[part], dst.at[me, part], sems.at[0, k, p], sems.at[1, k, p],
                        **{axis: ahead[k] * 2 + low},
                    )
                )
                slot = dst.at[behind[k] * 2 + low, part]
                self.second.append(
                    send(slot, slot, sems.at[2, k, p], sems.at[3, k, p], **{axis: partner})
                )
        self.at = 0

    def start(self):
        for p, copy in enumerate(self.own):
            if self.first:
                self.first[p].start()
            copy.start()
        for copy in self.first[self.pieces :]:
            copy.start()

    def start_piece(self, p):
        for copy in self.first[p :: self.pieces] + [self.own[p]]:
            copy.start()

    def forward_piece(self, p):
        for came, on in zip(self.first[p :: self.pieces], self.second[p :: self.pieces]):
            came.wait_recv()
            on.start()

    def arrive_piece(self, p):
        for copy in [self.own[p]] + self.second[p :: self.pieces]:
            copy.wait_recv()

    def forward(self, count):
        for _ in range(count):
            if self.at < len(self.first):
                self.first[self.at].wait_recv()
                self.second[self.at].start()
                self.at += 1

    def forward_all(self):
        self.forward(len(self.first))

    def arrive(self, k):
        copies = self.own if k == 0 else self.second[(k - 1) * self.pieces : k * self.pieces]
        for copy in copies:
            copy.wait_recv()

    def sent(self):
        for copy in self.first + self.own + self.second:
            copy.wait_send()


def run_tiles(first, last, step, carry):
    count = last - first
    unroll = 8 if count % 8 == 0 else 1
    return lax.fori_loop(first, last, step, carry, unroll=unroll)


F_TILE, F_OWNER, F_SUB, B_TILE, B_ROW, R_LAST, B_LAST = range(7)
R_SAME, B_SAME, R_SOME, B_SOME = range(4)


def forward_cuts(n, tiles, cap):
    cuts, waits = [], []
    for rank in range(1, n, 2):
        begin = max(0, tiles - cap * (n - rank))
        if begin > (cuts[-1] if cuts else 0):
            cuts.append(begin)
            waits.append([])
        if cuts:
            waits[-1].append(rank // 2)
    first = [k for k in range(n // 2) if all(k not in some for some in waits)]
    return [0] + cuts, [first] + waits


def fill_orders(n, blocks, cuts, rows_in, owner_in, sub_in, pad, table, flags):
    _, low, _, _, _ = places("dom", n)
    high = lax.axis_index("dom") // 2
    half = n // 2
    tp = pad.shape[1]
    tiles = owner_in.shape[1]
    pad[...] = jnp.zeros_like(pad)
    pad[0:1, 0:tiles] = rows_in[...]
    pad[1:2, 0:tiles] = owner_in[...]
    pad[2:3, 0:tiles] = sub_in[...]
    rows, owner, sub = pad[0:1, :], pad[1:2, :], pad[2:3, :]
    lane = lax.broadcasted_iota(jnp.int32, (tp, tp), 1)
    tile_row = lax.broadcasted_iota(jnp.int32, (1, tp), 1)
    valid = tile_row < tiles
    other = jnp.where(lax.rem(owner, 2) == low, 0, 1)
    owner_high = owner // 2
    arrival = lax.rem(high + half - owner_high, half) * 2 + other
    turn = lax.rem(owner_high + 2 * half - 1 - high, half)
    dest = ((1 - other) * half + turn) * blocks + sub

    def down(row):
        return jnp.broadcast_to(row, (tp, tp)).T

    def ranks(group):
        key = jnp.where(valid, group * tp + tile_row, (1 << 30) + tile_row)
        wide = jnp.broadcast_to(key, (tp, tp))
        before = jnp.where(wide < wide.T, 1, 0)
        group = jnp.broadcast_to(group, (tp, tp))
        alike = jnp.where(group == group.T, before, 0)
        place = jnp.sum(before, axis=1, keepdims=True)
        same = jnp.where(jnp.sum(alike, axis=1, keepdims=True) > 0, 1.0, 0.0)
        return place, same

    def put(ref, slot, rank, column):
        picked = jnp.where(rank == lane, column, jnp.zeros_like(column))
        ref[slot : slot + 1, 0:tp] = jnp.sum(picked, axis=0, keepdims=True)

    def ends(last_slot, some_slot, column, bound):
        lanes = lax.broadcasted_iota(jnp.int32, (tp, bound), 1)
        column = column[:, 0:1]
        upto = jnp.sum(jnp.where(column <= lanes, 1, 0), axis=0, keepdims=True)
        some = jnp.sum(jnp.where(column == lanes, 1, 0), axis=0, keepdims=True)
        table[last_slot : last_slot + 1, 0:bound] = jnp.maximum(upto - 1, 0)
        flags[some_slot : some_slot + 1, 0:bound] = jnp.where(some > 0, 1.0, 0.0)

    table[...] = jnp.zeros_like(table)
    flags[...] = jnp.zeros_like(flags)
    tile_col = down(tile_row)
    dest_col = down(jnp.where(valid, dest, 1 << 20))
    place, _ = ranks(arrival)
    group = jnp.zeros_like(place)
    for cut in cuts[1:]:
        group += jnp.where(place >= cut, 1, 0)
    by_group = jnp.broadcast_to(group, (tp, tp)).T[0:1, :] * blocks + rows
    by_row, same_row = ranks(by_group)
    put(table, F_TILE, by_row, tile_col)
    put(table, F_OWNER, by_row, down(owner))
    put(table, F_SUB, by_row, down(sub))
    put(flags, R_SAME, by_row, same_row)
    by_dest, same_dest = ranks(dest)
    put(table, B_TILE, by_dest, tile_col)
    put(table, B_ROW, by_dest, down(rows))
    put(flags, B_SAME, by_dest, same_dest)
    ends(R_LAST, R_SOME, down(jnp.where(valid, by_group, 1 << 20)), table.shape[1])
    ends(B_LAST, B_SOME, dest_col, table.shape[1])


def layer_kernel(
    n, f, embed, cot, weight, masks, rows_in, owner_in, sub_in, out, total, w_total,
    gath, ready, cot_all, w_all, agg, agg_all, out_all, scaled, inv_root, grad_agg, raw, narrow,
    own, pad, table, flags, order, marks, f_sums, b_sums, x_buf, z_buf, w_sum, w_buf,
    raw_sem, table_sem, e_sems, c_sems, w_sems, a_sems, r_sems, w_send, w_recv,
):
    me, low, partner, ahead, behind = places("dom", n)
    feat = lax.axis_index("feat")
    half = n // 2
    tiles, block, _ = masks.shape
    width, local_nodes = embed.shape
    blocks = local_nodes // block
    full = f * width
    cap = -(-2 * tiles // n)
    pieces = tiles // CHUNK
    spans = [pl.ds(c * CHUNK, CHUNK) for c in range(pieces)]
    loads = [
        pltpu.make_async_copy(masks.at[s], raw.at[s], raw_sem.at[c]) for c, s in enumerate(spans)
    ]
    for load in loads:
        load.start()
    greet(mates("dom", n), mates("feat", f))
    for b in range(blocks):
        own[b] = embed[:, b * block : (b + 1) * block]
    e_gather = Gather("dom", n, own, gath, e_sems, PIECES)
    c_gather = Gather("feat", f, cot, cot_all, c_sems, PIECES)
    w_gather = Gather("feat", f, weight, w_all, w_sems, 1)
    for gather in (e_gather, w_gather, c_gather):
        gather.start()
    ready[me] = own[...]
    cot_all[feat] = cot[...]
    w_all[feat] = weight[...]
    cuts, waits = forward_cuts(n, tiles, cap)
    fill_orders(n, blocks, cuts, rows_in, owner_in, sub_in, pad, table, flags)
    to_scalars = [
        pltpu.make_async_copy(table, order, table_sem.at[0]),
        pltpu.make_async_copy(flags, marks, table_sem.at[1]),
    ]
    for copy in to_scalars:
        copy.start()
    for c in range(pieces):
        loads[c].wait()

        @pl.loop(c * CHUNK, (c + 1) * CHUNK)
        def _(t):
            narrow[t] = raw[t].astype(jnp.float32).astype(jnp.bfloat16)

        e_gather.forward(1)
    w_gather.forward_all()
    e_gather.forward_all()
    c_gather.forward_all()
    for copy in to_scalars:
        copy.wait()

    for k in range(1, half):
        ready[behind[k] * 2 + low] = gath[behind[k] * 2 + low]
    ones = jnp.ones((ONES, block), jnp.bfloat16)

    def forward_tile(k, held):
        taken = ready[order[F_OWNER, k], order[F_SUB, k]]
        held = held * marks[R_SAME, k] + lax.dot_general(
            jnp.concatenate([taken, ones], axis=0),
            narrow[order[F_TILE, k]],
            (((1,), (1,)), ((), ())),
            preferred_element_type=jnp.float32,
        )
        f_sums[k] = held
        return held

    held = jnp.zeros((width + ONES, block), jnp.float32)
    for begin, end, arriving in zip(cuts, cuts[1:] + [tiles], waits):
        for k in arriving:
            e_gather.arrive(k)
            source = behind[k] * 2 + 1 - low
            ready[source] = gath[source]
        held = run_tiles(begin, end, forward_tile, held)

    def segment(sums, last, some, b):
        return sums[order[last, b]] * marks[some, b]

    a_gather = Gather("feat", f, agg, agg_all, a_sems, PIECES)
    group = blocks // PIECES
    step = group * block
    for b in range(blocks):
        columns = slice(b * block, (b + 1) * block)
        value = segment(f_sums, R_LAST, R_SOME, b)
        for g in range(1, len(cuts)):
            value += segment(f_sums, R_LAST, R_SOME, g * blocks + b)
        root = 1.0 / jnp.sqrt(1.0 + value[width : width + 1, :])
        inv_root[:, columns] = root
        agg[b] = (embed[:, columns].astype(jnp.float32) + value[:width, :] * root).astype(
            jnp.bfloat16
        )
        if (b + 1) % group == 0:
            a_gather.start_piece(b // group)
    agg_all[feat] = agg[...]
    for k in range(f // 2):
        w_gather.arrive(k)
        c_gather.arrive(k)
    whole_w = w_all[...].reshape(full, full)

    def dense(p):
        columns = slice(p * step, (p + 1) * step)
        held = range(p * group, (p + 1) * group)
        values = jnp.concatenate([agg_all[:, b].reshape(full, block) for b in held], axis=1)
        pre = lax.dot_general(
            whole_w, values, (((0,), (0,)), ((), ())), preferred_element_type=jnp.float32
        )
        gate = jax.nn.sigmoid(pre)
        out_all[:, :, columns] = (pre * gate).astype(jnp.bfloat16).reshape(f, width, step)
        given = cot_all[:, :, columns].reshape(full, step).astype(jnp.float32)
        grad = (given * gate * (1.0 + pre * (1.0 - gate))).astype(jnp.bfloat16)
        back = jnp.dot(weight[...], grad, preferred_element_type=jnp.float32)
        grad_agg[:, columns] = back
        narrowed = (back * inv_root[:, columns]).astype(jnp.bfloat16)
        for i, b in enumerate(held):
            scaled[b] = narrowed[:, i * block : (i + 1) * block]
        terms = lax.dot_general(
            jnp.concatenate([agg[b] for b in held], axis=1),
            grad,
            (((1,), (1,)), ((), ())),
            preferred_element_type=jnp.float32,
        )
        if p:
            w_sum[0] += terms
        else:
            w_sum[0] = terms

    a_gather.forward_piece(0)
    for p in range(PIECES):
        if p + 1 < PIECES:
            a_gather.forward_piece(p + 1)
        a_gather.arrive_piece(p)
        dense(p)

    rounds = n.bit_length() - 1
    w_copies = []
    for b in range(rounds):
        bit = lax.rem(me // (1 << b), 2)
        mate = me + (1 - 2 * bit) * (1 << b)
        w_copies.append(send(w_sum.at[b], w_buf.at[b], w_send.at[b], w_recv.at[b], dom=mate))
    w_copies[0].start()

    def w_round(b):
        w_copies[b].wait_recv()
        summed = w_sum[b] + w_buf[b]
        if b == rounds - 1:
            w_total[...] = summed * (1.0 / math.sqrt(n * local_nodes))
        else:
            w_sum[b + 1] = summed
            w_copies[b + 1].start()

    turns = list(range(1, half)) + [0]
    parts = [pl.ds(p * group, group) for p in range(PIECES)]
    x_out, z_out = ready.at[pl.ds(0, half)], ready.at[pl.ds(half, half)]
    x_copies = {
        (k, p): send(
            x_out.at[k, part], x_buf.at[k, part], r_sems.at[0, k, p], r_sems.at[1, k, p],
            dom=partner,
        )
        for k in turns
        for p, part in enumerate(parts)
    }
    z_copies = {
        (k, p): send(
            z_out.at[k, part], z_buf.at[k, part], r_sems.at[2, k, p], r_sems.at[3, k, p],
            dom=ahead[k] * 2 + low,
        )
        for k in turns[:-1]
        for p, part in enumerate(parts)
    }

    def backward_tile(k, held):
        held = held * marks[B_SAME, k] + jnp.dot(
            scaled[order[B_ROW, k]],
            narrow[order[B_TILE, k]],
            preferred_element_type=jnp.float32,
        )
        b_sums[k] = held
        return held

    held = jnp.zeros((width, block), jnp.float32)
    at = 0
    for j, k in enumerate(turns):
        upto = min(tiles, cap * (j + 1)) if j < half - 1 else tiles
        held = run_tiles(at, upto, backward_tile, held)
        at = upto
        for b in range(blocks):
            value = segment(b_sums, B_LAST, B_SOME, j * blocks + b)
            x_out[k, b] = value.astype(jnp.bfloat16)
        for p in range(PIECES):
            x_copies[k, p].start()
    for j, k in enumerate(turns):
        for b in range(blocks):
            columns = slice(b * block, (b + 1) * block)
            value = segment(b_sums, B_LAST, B_SOME, (half + j) * blocks + b)
            if k:
                z_out[k, b] = value.astype(jnp.bfloat16)
            else:
                total[:, columns] = grad_agg[:, columns] + value
    out[...] = out_all[feat]
    for j, k in enumerate(turns):
        for p, part in enumerate(parts):
            x_copies[k, p].wait_recv()
            for b in range(p * group, (p + 1) * group):
                came = x_buf[k, b].astype(jnp.float32)
                if k:
                    z_out[k, b] = (z_out[k, b].astype(jnp.float32) + came).astype(jnp.bfloat16)
                else:
                    total[:, b * block : (b + 1) * block] += came
            if k:
                z_copies[k, p].start()
        if j < rounds:
            w_round(j)
    for b in range(half, rounds):
        w_round(b)
    for k in turns[:-1]:
        for p, part in enumerate(parts):
            z_copies[k, p].wait_recv()
            for b in range(p * group, (p + 1) * group):
                total[:, b * block : (b + 1) * block] += z_buf[k, b].astype(jnp.float32)
    for gather in (e_gather, w_gather, c_gather, a_gather):
        gather.sent()
    for copy in list(x_copies.values()) + list(z_copies.values()) + w_copies:
        copy.wait_send()


def finish_kernel(out, total, w_total, output, embed_grad, weight_grad):
    output[...] = out[...]
    embed_grad[...] = total[...]
    weight_grad[...] = w_total[...]


def params(collective_id=None):
    if collective_id is None:
        return pltpu.CompilerParams(vmem_limit_bytes=VMEM_LIMIT)
    return pltpu.CompilerParams(
        collective_id=collective_id, has_side_effects=True, vmem_limit_bytes=VMEM_LIMIT
    )


def per_device(embed, weight, cotangent, edge_masks, tile_rows, tile_owner, tile_sub):
    width, local_nodes = embed.shape
    tiles, block, _ = edge_masks.shape
    blocks = local_nodes // block
    n = lax.axis_size("dom")
    f = lax.axis_size("feat")
    full = f * width
    half = n // 2
    rounds = n.bit_length() - 1
    bf, f32 = jnp.bfloat16, jnp.float32
    dma = pltpu.SemaphoreType.DMA
    lanes = -(-tiles // 128) * 128
    table = (8, max(lanes, -(-n * blocks // 128) * 128))
    shard = (width, local_nodes)

    results = (
        jax.ShapeDtypeStruct(shard, bf),
        jax.ShapeDtypeStruct(shard, f32),
        jax.ShapeDtypeStruct((width, full), f32),
    )
    layer = pl.pallas_call(
        functools.partial(layer_kernel, n, f),
        out_shape=results,
        in_specs=[VMEM, VMEM, VMEM, ANY, VMEM, VMEM, VMEM],
        out_specs=(VMEM,) * 3,
        scratch_shapes=[
            pltpu.VMEM((n, blocks, width, block), bf),
            pltpu.VMEM((n, blocks, width, block), bf),
            pltpu.VMEM((f, *shard), bf),
            pltpu.VMEM((f, width, full), bf),
            pltpu.VMEM((blocks, width, block), bf),
            pltpu.VMEM((f, blocks, width, block), bf),
            pltpu.VMEM((f, *shard), bf),
            pltpu.VMEM((blocks, width, block), bf),
            pltpu.VMEM((1, local_nodes), f32),
            pltpu.VMEM(shard, f32),
            pltpu.VMEM((tiles, block, block), jnp.int32),
            pltpu.VMEM((tiles, block, block), bf),
            pltpu.VMEM((blocks, width, block), bf),
            pltpu.VMEM((8, lanes), jnp.int32),
            pltpu.VMEM(table, jnp.int32),
            pltpu.VMEM(table, f32),
            pltpu.SMEM(table, jnp.int32),
            pltpu.SMEM(table, f32),
            pltpu.VMEM((tiles, width + ONES, block), f32),
            pltpu.VMEM((tiles, width, block), f32),
            pltpu.VMEM((half, blocks, width, block), bf),
            pltpu.VMEM((half, blocks, width, block), bf),
            pltpu.VMEM((rounds, width, full), f32),
            pltpu.VMEM((rounds, width, full), f32),
            dma((tiles // CHUNK,)),
            dma((2,)),
            dma((4, half, PIECES)),
            dma((4, f // 2, PIECES)),
            dma((4, f // 2, 1)),
            dma((4, f // 2, PIECES)),
            dma((4, half, PIECES)),
            dma((rounds,)),
            dma((rounds,)),
        ],
        compiler_params=params(0),
        name="layer",
    )(
        embed, cotangent, weight, edge_masks,
        tile_rows.reshape(1, tiles), tile_owner.reshape(1, tiles), tile_sub.reshape(1, tiles),
    )
    output, embed_grad, weight_grad = pl.pallas_call(
        finish_kernel,
        out_shape=results,
        in_specs=[VMEM] * 3,
        out_specs=(VMEM,) * 3,
        compiler_params=params(),
        name="finish",
    )(*layer)
    return (output, embed_grad, weight_grad)


def solution(mesh):
    in_specs = (
        P("feat", "dom"),
        P("feat", None),
        P("feat", "dom"),
        P("dom", None, None),
        P("dom"),
        P("dom", None),
        P("dom"),
    )
    out_specs = (P("feat", "dom"), P("feat", "dom"), P("feat", None))
    return jax.shard_map(
        per_device, mesh=mesh, in_specs=in_specs, out_specs=out_specs, check_vma=False
    )
```

```python
import functools
import math

import jax
import jax.numpy as jnp
from jax import lax
from jax.experimental import pallas as pl
from jax.experimental.pallas import tpu as pltpu
from jax.sharding import PartitionSpec as P

MESH = pl.DeviceIdType.MESH
VMEM = pl.BlockSpec(memory_space=pltpu.VMEM)
ANY = pl.BlockSpec(memory_space=pl.ANY)
ONES = 16
CHUNK = 16
PIECES = 4
VMEM_LIMIT = 56 * 1024 * 1024


def greet(dom_mates, feat_mates):
    barrier = pltpu.get_barrier_semaphore()
    for mate in dom_mates:
        pl.semaphore_signal(barrier, inc=1, device_id={"dom": mate}, device_id_type=MESH)
    for mate in feat_mates:
        pl.semaphore_signal(barrier, inc=1, device_id={"feat": mate}, device_id_type=MESH)
    pl.semaphore_wait(barrier, len(dom_mates) + len(feat_mates))


def send(src, dst, send_sem, recv_sem, **where):
    return pltpu.make_async_remote_copy(
        src_ref=src,
        dst_ref=dst,
        send_sem=send_sem,
        recv_sem=recv_sem,
        device_id=where,
        device_id_type=MESH,
    )


def places(axis, n):
    me = lax.axis_index(axis)
    half = n // 2
    high, low = me // 2, lax.rem(me, 2)
    ahead = [lax.rem(high + k, half) for k in range(half)]
    behind = [lax.rem(high + half - k, half) for k in range(half)]
    return me, low, me + 1 - 2 * low, ahead, behind


def mates(axis, n):
    _, low, partner, ahead, _ = places(axis, n)
    return [ahead[k] * 2 + low for k in range(1, n // 2)] + [partner]


class Gather:
    def __init__(self, axis, n, src, dst, sems, pieces):
        me, low, partner, ahead, behind = places(axis, n)
        half = n // 2
        rows = src.shape[0] // pieces
        self.pieces = pieces
        self.first, self.second, self.own = [], [], []
        spans = [pl.ds(p * rows, rows) for p in range(pieces)]
        for p, part in enumerate(spans):
            self.own.append(
                send(
                    src.at[part], dst.at[me, part], sems.at[2, 0, p], sems.at[3, 0, p],
                    **{axis: partner},
                )
            )
        for k in range(1, half):
            for p, part in enumerate(spans):
                self.first.append(
                    send(
                        src.at[part], dst.at[me, part], sems.at[0, k, p], sems.at[1, k, p],
                        **{axis: ahead[k] * 2 + low},
                    )
                )
                slot = dst.at[behind[k] * 2 + low, part]
                self.second.append(
                    send(slot, slot, sems.at[2, k, p], sems.at[3, k, p], **{axis: partner})
                )
        self.at = 0

    def start(self):
        for p, copy in enumerate(self.own):
            if self.first:
                self.first[p].start()
            copy.start()
        for copy in self.first[self.pieces :]:
            copy.start()

    def start_piece(self, p):
        for copy in self.first[p :: self.pieces] + [self.own[p]]:
            copy.start()

    def forward_piece(self, p):
        for came, on in zip(self.first[p :: self.pieces], self.second[p :: self.pieces]):
            came.wait_recv()
            on.start()

    def arrive_piece(self, p):
        for copy in [self.own[p]] + self.second[p :: self.pieces]:
            copy.wait_recv()

    def forward(self, count):
        for _ in range(count):
            if self.at < len(self.first):
                self.first[self.at].wait_recv()
                self.second[self.at].start()
                self.at += 1

    def forward_all(self):
        self.forward(len(self.first))

    def arrive(self, k):
        copies = self.own if k == 0 else self.second[(k - 1) * self.pieces : k * self.pieces]
        for copy in copies:
            copy.wait_recv()

    def sent(self):
        for copy in self.first + self.own + self.second:
            copy.wait_send()


def run_tiles(first, last, step, carry):
    count = last - first
    unroll = 8 if count % 8 == 0 else 1
    return lax.fori_loop(first, last, step, carry, unroll=unroll)


F_TILE, F_OWNER, F_SUB, B_TILE, B_ROW, R_LAST, B_LAST = range(7)
R_SAME, B_SAME, R_SOME, B_SOME = range(4)


def forward_cuts(n, tiles, cap):
    cuts, waits = [], []
    for rank in range(1, n, 2):
        begin = max(0, tiles - cap * (n - rank))
        if begin > (cuts[-1] if cuts else 0):
            cuts.append(begin)
            waits.append([])
        if cuts:
            waits[-1].append(rank // 2)
    first = [k for k in range(n // 2) if all(k not in some for some in waits)]
    return [0] + cuts, [first] + waits


def fill_orders(n, blocks, cuts, rows_in, owner_in, sub_in, pad, table, flags):
    _, low, _, _, _ = places("dom", n)
    high = lax.axis_index("dom") // 2
    half = n // 2
    tp = pad.shape[1]
    tiles = owner_in.shape[1]
    pad[...] = jnp.zeros_like(pad)
    pad[0:1, 0:tiles] = rows_in[...]
    pad[1:2, 0:tiles] = owner_in[...]
    pad[2:3, 0:tiles] = sub_in[...]
    rows, owner, sub = pad[0:1, :], pad[1:2, :], pad[2:3, :]
    lane = lax.broadcasted_iota(jnp.int32, (tp, tp), 1)
    tile_row = lax.broadcasted_iota(jnp.int32, (1, tp), 1)
    valid = tile_row < tiles
    other = jnp.where(lax.rem(owner, 2) == low, 0, 1)
    owner_high = owner // 2
    arrival = lax.rem(high + half - owner_high, half) * 2 + other
    turn = lax.rem(owner_high + 2 * half - 1 - high, half)
    dest = ((1 - other) * half + turn) * blocks + sub

    def down(row):
        return jnp.broadcast_to(row, (tp, tp)).T

    def ranks(group):
        key = jnp.where(valid, group * tp + tile_row, (1 << 30) + tile_row)
        wide = jnp.broadcast_to(key, (tp, tp))
        before = jnp.where(wide < wide.T, 1, 0)
        group = jnp.broadcast_to(group, (tp, tp))
        alike = jnp.where(group == group.T, before, 0)
        place = jnp.sum(before, axis=1, keepdims=True)
        same = jnp.where(jnp.sum(alike, axis=1, keepdims=True) > 0, 1.0, 0.0)
        return place, same

    def put(ref, slot, rank, column):
        picked = jnp.where(rank == lane, column, jnp.zeros_like(column))
        ref[slot : slot + 1, 0:tp] = jnp.sum(picked, axis=0, keepdims=True)

    def ends(last_slot, some_slot, column, bound):
        lanes = lax.broadcasted_iota(jnp.int32, (tp, bound), 1)
        column = column[:, 0:1]
        upto = jnp.sum(jnp.where(column <= lanes, 1, 0), axis=0, keepdims=True)
        some = jnp.sum(jnp.where(column == lanes, 1, 0), axis=0, keepdims=True)
        table[last_slot : last_slot + 1, 0:bound] = jnp.maximum(upto - 1, 0)
        flags[some_slot : some_slot + 1, 0:bound] = jnp.where(some > 0, 1.0, 0.0)

    table[...] = jnp.zeros_like(table)
    flags[...] = jnp.zeros_like(flags)
    tile_col = down(tile_row)
    dest_col = down(jnp.where(valid, dest, 1 << 20))
    place, _ = ranks(arrival)
    group = jnp.zeros_like(place)
    for cut in cuts[1:]:
        group += jnp.where(place >= cut, 1, 0)
    by_group = jnp.broadcast_to(group, (tp, tp)).T[0:1, :] * blocks + rows
    by_row, same_row = ranks(by_group)
    put(table, F_TILE, by_row, tile_col)
    put(table, F_OWNER, by_row, down(owner))
    put(table, F_SUB, by_row, down(sub))
    put(flags, R_SAME, by_row, same_row)
    by_dest, same_dest = ranks(dest)
    put(table, B_TILE, by_dest, tile_col)
    put(table, B_ROW, by_dest, down(rows))
    put(flags, B_SAME, by_dest, same_dest)
    ends(R_LAST, R_SOME, down(jnp.where(valid, by_group, 1 << 20)), table.shape[1])
    ends(B_LAST, B_SOME, dest_col, table.shape[1])


def layer_kernel(
    n, f, embed, cot, weight, masks, rows_in, owner_in, sub_in, out, total, w_total,
    gath, ready, cot_all, w_all, agg, agg_all, out_all, scaled, inv_root, grad_agg, raw, narrow,
    own, pad, table, flags, order, marks, f_sums, b_sums, x_buf, z_buf, w_sum, w_buf,
    raw_sem, table_sem, e_sems, c_sems, w_sems, a_sems, r_sems, w_send, w_recv,
):
    me, low, partner, ahead, behind = places("dom", n)
    feat = lax.axis_index("feat")
    half = n // 2
    tiles, block, _ = masks.shape
    width, local_nodes = embed.shape
    blocks = local_nodes // block
    full = f * width
    cap = -(-2 * tiles // n)
    pieces = tiles // CHUNK
    spans = [pl.ds(c * CHUNK, CHUNK) for c in range(pieces)]
    loads = [
        pltpu.make_async_copy(masks.at[s], raw.at[s], raw_sem.at[c]) for c, s in enumerate(spans)
    ]
    for load in loads:
        load.start()
    greet(mates("dom", n), mates("feat", f))
    for b in range(blocks):
        own[b] = embed[:, b * block : (b + 1) * block]
    e_gather = Gather("dom", n, own, gath, e_sems, PIECES)
    c_gather = Gather("feat", f, cot, cot_all, c_sems, PIECES)
    w_gather = Gather("feat", f, weight, w_all, w_sems, 1)
    for gather in (e_gather, w_gather, c_gather):
        gather.start()
    ready[me] = own[...]
    cot_all[feat] = cot[...]
    w_all[feat] = weight[...]
    cuts, waits = forward_cuts(n, tiles, cap)
    fill_orders(n, blocks, cuts, rows_in, owner_in, sub_in, pad, table, flags)
    to_scalars = [
        pltpu.make_async_copy(table, order, table_sem.at[0]),
        pltpu.make_async_copy(flags, marks, table_sem.at[1]),
    ]
    for copy in to_scalars:
        copy.start()
    for c in range(pieces):
        loads[c].wait()

        @pl.loop(c * CHUNK, (c + 1) * CHUNK)
        def _(t):
            narrow[t] = raw[t].astype(jnp.float32).astype(jnp.bfloat16)

        e_gather.forward(1)
    w_gather.forward_all()
    e_gather.forward_all()
    c_gather.forward_all()
    for copy in to_scalars:
        copy.wait()

    for k in range(1, half):
        ready[behind[k] * 2 + low] = gath[behind[k] * 2 + low]
    ones = jnp.ones((ONES, block), jnp.bfloat16)

    def forward_tile(k, held):
        taken = ready[order[F_OWNER, k], order[F_SUB, k]]
        held = held * marks[R_SAME, k] + lax.dot_general(
            jnp.concatenate([taken, ones], axis=0),
            narrow[order[F_TILE, k]],
            (((1,), (1,)), ((), ())),
            preferred_element_type=jnp.float32,
        )
        f_sums[k] = held
        return held

    held = jnp.zeros((width + ONES, block), jnp.float32)
    for begin, end, arriving in zip(cuts, cuts[1:] + [tiles], waits):
        for k in arriving:
            e_gather.arrive(k)
            source = behind[k] * 2 + 1 - low
            ready[source] = gath[source]
        held = run_tiles(begin, end, forward_tile, held)

    def segment(sums, last, some, b):
        return sums[order[last, b]] * marks[some, b]

    a_gather = Gather("feat", f, agg, agg_all, a_sems, PIECES)
    group = blocks // PIECES
    step = group * block
    for b in range(blocks):
        columns = slice(b * block, (b + 1) * block)
        value = segment(f_sums, R_LAST, R_SOME, b)
        for g in range(1, len(cuts)):
            value += segment(f_sums, R_LAST, R_SOME, g * blocks + b)
        root = 1.0 / jnp.sqrt(1.0 + value[width : width + 1, :])
        inv_root[:, columns] = root
        agg[b] = (embed[:, columns].astype(jnp.float32) + value[:width, :] * root).astype(
            jnp.bfloat16
        )
        if (b + 1) % group == 0:
            a_gather.start_piece(b // group)
    agg_all[feat] = agg[...]
    for k in range(f // 2):
        w_gather.arrive(k)
        c_gather.arrive(k)
    whole_w = w_all[...].reshape(full, full)

    def dense(p):
        columns = slice(p * step, (p + 1) * step)
        held = range(p * group, (p + 1) * group)
        values = jnp.concatenate([agg_all[:, b].reshape(full, block) for b in held], axis=1)
        pre = lax.dot_general(
            whole_w, values, (((0,), (0,)), ((), ())), preferred_element_type=jnp.float32
        )
        gate = jax.nn.sigmoid(pre)
        out_all[:, :, columns] = (pre * gate).astype(jnp.bfloat16).reshape(f, width, step)
        given = cot_all[:, :, columns].reshape(full, step).astype(jnp.float32)
        grad = (given * gate * (1.0 + pre * (1.0 - gate))).astype(jnp.bfloat16)
        back = jnp.dot(weight[...], grad, preferred_element_type=jnp.float32)
        grad_agg[:, columns] = back
        narrowed = (back * inv_root[:, columns]).astype(jnp.bfloat16)
        for i, b in enumerate(held):
            scaled[b] = narrowed[:, i * block : (i + 1) * block]
        terms = lax.dot_general(
            jnp.concatenate([agg[b] for b in held], axis=1),
            grad,
            (((1,), (1,)), ((), ())),
            preferred_element_type=jnp.float32,
        )
        if p:
            w_sum[0] += terms
        else:
            w_sum[0] = terms

    a_gather.forward_piece(0)
    for p in range(PIECES):
        if p + 1 < PIECES:
            a_gather.forward_piece(p + 1)
        a_gather.arrive_piece(p)
        dense(p)

    rounds = n.bit_length() - 1
    w_copies = []
    for b in range(rounds):
        bit = lax.rem(me // (1 << b), 2)
        mate = me + (1 - 2 * bit) * (1 << b)
        w_copies.append(send(w_sum.at[b], w_buf.at[b], w_send.at[b], w_recv.at[b], dom=mate))

    def w_round(b):
        w_copies[b].wait_recv()
        summed = w_sum[b] + w_buf[b]
        if b == rounds - 1:
            w_total[...] = summed * (1.0 / math.sqrt(n * local_nodes))
        else:
            w_sum[b + 1] = summed
            w_copies[b + 1].start()

    turns = list(range(1, half)) + [0]
    parts = [pl.ds(p * group, group) for p in range(PIECES)]
    x_out, z_out = ready.at[pl.ds(0, half)], ready.at[pl.ds(half, half)]
    x_copies = {
        (k, p): send(
            x_out.at[k, part], x_buf.at[k, part], r_sems.at[0, k, p], r_sems.at[1, k, p],
            dom=partner,
        )
        for k in turns
        for p, part in enumerate(parts)
    }
    z_copies = {
        (k, p): send(
            z_out.at[k, part], z_buf.at[k, part], r_sems.at[2, k, p], r_sems.at[3, k, p],
            dom=ahead[k] * 2 + low,
        )
        for k in turns[:-1]
        for p, part in enumerate(parts)
    }

    def backward_tile(k, held):
        held = held * marks[B_SAME, k] + jnp.dot(
            scaled[order[B_ROW, k]],
            narrow[order[B_TILE, k]],
            preferred_element_type=jnp.float32,
        )
        b_sums[k] = held
        return held

    held = jnp.zeros((width, block), jnp.float32)
    at = 0
    for j, k in enumerate(turns):
        upto = min(tiles, cap * (j + 1)) if j < half - 1 else tiles
        held = run_tiles(at, upto, backward_tile, held)
        at = upto
        for b in range(blocks):
            value = segment(b_sums, B_LAST, B_SOME, j * blocks + b)
            x_out[k, b] = value.astype(jnp.bfloat16)
        for p in range(PIECES):
            x_copies[k, p].start()
        if j == min(1, half - 1):
            w_copies[0].start()
    for j, k in enumerate(turns):
        for b in range(blocks):
            columns = slice(b * block, (b + 1) * block)
            value = segment(b_sums, B_LAST, B_SOME, (half + j) * blocks + b)
            if k:
                z_out[k, b] = value.astype(jnp.bfloat16)
            else:
                total[:, columns] = grad_agg[:, columns] + value
    out[...] = out_all[feat]
    for j, k in enumerate(turns):
        for p, part in enumerate(parts):
            x_copies[k, p].wait_recv()
            for b in range(p * group, (p + 1) * group):
                came = x_buf[k, b].astype(jnp.float32)
                if k:
                    z_out[k, b] = (z_out[k, b].astype(jnp.float32) + came).astype(jnp.bfloat16)
                else:
                    total[:, b * block : (b + 1) * block] += came
            if k:
                z_copies[k, p].start()
        if j < rounds:
            w_round(j)
    for b in range(half, rounds):
        w_round(b)
    for k in turns[:-1]:
        for p, part in enumerate(parts):
            z_copies[k, p].wait_recv()
            for b in range(p * group, (p + 1) * group):
                total[:, b * block : (b + 1) * block] += z_buf[k, b].astype(jnp.float32)
    for gather in (e_gather, w_gather, c_gather, a_gather):
        gather.sent()
    for copy in list(x_copies.values()) + list(z_copies.values()) + w_copies:
        copy.wait_send()


def finish_kernel(out, total, w_total, output, embed_grad, weight_grad):
    output[...] = out[...]
    embed_grad[...] = total[...]
    weight_grad[...] = w_total[...]


def params(collective_id=None):
    if collective_id is None:
        return pltpu.CompilerParams(vmem_limit_bytes=VMEM_LIMIT)
    return pltpu.CompilerParams(
        collective_id=collective_id, has_side_effects=True, vmem_limit_bytes=VMEM_LIMIT
    )


def per_device(embed, weight, cotangent, edge_masks, tile_rows, tile_owner, tile_sub):
    width, local_nodes = embed.shape
    tiles, block, _ = edge_masks.shape
    blocks = local_nodes // block
    n = lax.axis_size("dom")
    f = lax.axis_size("feat")
    full = f * width
    half = n // 2
    rounds = n.bit_length() - 1
    bf, f32 = jnp.bfloat16, jnp.float32
    dma = pltpu.SemaphoreType.DMA
    lanes = -(-tiles // 128) * 128
    table = (8, max(lanes, -(-n * blocks // 128) * 128))
    shard = (width, local_nodes)

    results = (
        jax.ShapeDtypeStruct(shard, bf),
        jax.ShapeDtypeStruct(shard, f32),
        jax.ShapeDtypeStruct((width, full), f32),
    )
    layer = pl.pallas_call(
        functools.partial(layer_kernel, n, f),
        out_shape=results,
        in_specs=[VMEM, VMEM, VMEM, ANY, VMEM, VMEM, VMEM],
        out_specs=(VMEM,) * 3,
        scratch_shapes=[
            pltpu.VMEM((n, blocks, width, block), bf),
            pltpu.VMEM((n, blocks, width, block), bf),
            pltpu.VMEM((f, *shard), bf),
            pltpu.VMEM((f, width, full), bf),
            pltpu.VMEM((blocks, width, block), bf),
            pltpu.VMEM((f, blocks, width, block), bf),
            pltpu.VMEM((f, *shard), bf),
            pltpu.VMEM((blocks, width, block), bf),
            pltpu.VMEM((1, local_nodes), f32),
            pltpu.VMEM(shard, f32),
            pltpu.VMEM((tiles, block, block), jnp.int32),
            pltpu.VMEM((tiles, block, block), bf),
            pltpu.VMEM((blocks, width, block), bf),
            pltpu.VMEM((8, lanes), jnp.int32),
            pltpu.VMEM(table, jnp.int32),
            pltpu.VMEM(table, f32),
            pltpu.SMEM(table, jnp.int32),
            pltpu.SMEM(table, f32),
            pltpu.VMEM((tiles, width + ONES, block), f32),
            pltpu.VMEM((tiles, width, block), f32),
            pltpu.VMEM((half, blocks, width, block), bf),
            pltpu.VMEM((half, blocks, width, block), bf),
            pltpu.VMEM((rounds, width, full), f32),
            pltpu.VMEM((rounds, width, full), f32),
            dma((tiles // CHUNK,)),
            dma((2,)),
            dma((4, half, PIECES)),
            dma((4, f // 2, PIECES)),
            dma((4, f // 2, 1)),
            dma((4, f // 2, PIECES)),
            dma((4, half, PIECES)),
            dma((rounds,)),
            dma((rounds,)),
        ],
        compiler_params=params(0),
        name="layer",
    )(
        embed, cotangent, weight, edge_masks,
        tile_rows.reshape(1, tiles), tile_owner.reshape(1, tiles), tile_sub.reshape(1, tiles),
    )
    output, embed_grad, weight_grad = pl.pallas_call(
        finish_kernel,
        out_shape=results,
        in_specs=[VMEM] * 3,
        out_specs=(VMEM,) * 3,
        compiler_params=params(),
        name="finish",
    )(*layer)
    return (output, embed_grad, weight_grad)


def solution(mesh):
    in_specs = (
        P("feat", "dom"),
        P("feat", None),
        P("feat", "dom"),
        P("dom", None, None),
        P("dom"),
        P("dom", None),
        P("dom"),
    )
    out_specs = (P("feat", "dom"), P("feat", "dom"), P("feat", None))
    return jax.shard_map(
        per_device, mesh=mesh, in_specs=in_specs, out_specs=out_specs, check_vma=False
    )
```
